256 devices in a mesh: dp: 4 (over x_lo, core), mx: 16 (over z, x_hi), my: 4 (over y).
Axes of the slice: x: 4 (x_hi: 2, x_lo: 2; x = x_hi * 2 + x_lo), y: 4, z: 8, core: 2. Of those that a mesh axis runs over, the one named last changes fastest.
Arguments:
- normed: bfloat16 [2048, 6144], P('dp', 'mx'), may hold values from -6 to 6
- out_grad: bfloat16 [2048, 6144], P('dp', 'mx'), may hold values from -6 to 6
- w_in: bfloat16 [6144, 12288], P('mx', ('my', 'dp')), may hold values from -0.078125 to 0.078125
- w_out: bfloat16 [12288, 6144], P(('my', 'dp'), 'mx'), may hold values from -0.0546875 to 0.0546875
- first_in: float32 [6144, 12288], P('mx', ('my', 'dp')), may hold values from -6 to 6
- second_in: float32 [6144, 12288], P('mx', ('my', 'dp')), may hold values from 0.5 to 8
- first_out: float32 [12288, 6144], P(('my', 'dp'), 'mx'), may hold values from -6 to 6
- second_out: float32 [12288, 6144], P(('my', 'dp'), 'mx'), may hold values from 0.5 to 8
Outputs:
- input_grad: bfloat16 [2048, 6144], P(('dp', 'my'), 'mx')
- update_in: bfloat16 [6144, 12288], P('mx', ('my', 'dp'))
- new_first_in: float32 [6144, 12288], P('mx', ('my', 'dp'))
- new_second_in: float32 [6144, 12288], P('mx', ('my', 'dp'))
- update_out: bfloat16 [12288, 6144], P(('my', 'dp'), 'mx')
- new_first_out: float32 [12288, 6144], P(('my', 'dp'), 'mx')
- new_second_out: float32 [12288, 6144], P(('my', 'dp'), 'mx')
The draws below stay inside these ranges and needn't reach their ends.
All inputs are finite; a program needn't handle non-finite values.
Results may differ from the reference program's by a relative error of at most 0.027.
Values may be sent and summed in bfloat16 or wider, within the bound.
No kernel may reach another device: no remote copies, remote signals or barrier semaphores. Data moves between devices by JAX's collectives and lax.ppermute only.
A program may use at most 128 MiB of HBM per device.

```python
import math
import jax
import jax.numpy as jnp
from jax import lax

D = 6144
FFW = 12288
TOKENS = 2048
IMAGES = 8
N_MX = 16


def shard_levels(stream_key, extent, pieces, least, largest):
    level = 1.0
    for dim, parts in pieces:
        draws = jax.random.uniform(jax.random.fold_in(jax.random.fold_in(stream_key, 6), dim), (parts,), jnp.float32, least / len(pieces), largest / len(pieces))
        level = level * jnp.repeat(jnp.exp(draws), extent[dim] // parts).reshape((-1,) + (1,) * (len(extent) - 1 - dim))
    return level


def centred(rng, extent, scale, reach, shards=(), held_as=jnp.bfloat16):
    level = shard_levels(rng, extent, shards, -0.22, 0.18) if shards else 1.0
    drawn = jax.random.normal(rng, extent, jnp.float32) * scale * level
    return jnp.minimum(jnp.maximum(drawn, -reach), reach).astype(held_as)


def setup_inputs(seed: int = 0) -> dict:
    arg_keys = jax.random.split(jax.random.key(seed), 9)
    return {
        "normed": centred(arg_keys[0], (TOKENS, D), 1.0, 6.0, ((0, 4), (1, 16))),
        "out_grad": centred(arg_keys[1], (TOKENS, D), 1.0, 6.0, ((0, 4), (1, 16))),
        "w_in": centred(arg_keys[2], (D, FFW), D ** -0.5, 0.078125, ((0, 16), (1, 16))),
        "w_out": centred(arg_keys[3], (FFW, D), FFW ** -0.5, 0.0546875, ((0, 16), (1, 16))),
        "first_in": centred(arg_keys[4], (D, FFW), 1.0, 6.0, ((0, 16), (1, 16)), jnp.float32),
        "second_in": jnp.clip(jnp.exp(math.log(8.0) - 2.7725887 * jax.random.uniform(arg_keys[5], (D, FFW), jnp.float32) ** shard_levels(arg_keys[5], (D, FFW), ((0, 16), (1, 16)), -0.2, 0.2)), 0.5, 8.0),
        "first_out": centred(arg_keys[6], (FFW, D), 1.0, 6.0, ((0, 16), (1, 16)), jnp.float32),
        "second_out": jnp.clip(jnp.exp(math.log(8.0) - 2.7725887 * jax.random.uniform(arg_keys[7], (FFW, D), jnp.float32) ** shard_levels(arg_keys[7], (FFW, D), ((0, 16), (1, 16)), -0.2, 0.2)), 0.5, 8.0),
    }


INV_ROOT2 = 0.7071067811865476
INV_ROOT2PI = 0.3989422804014327
FIRST_FIX = 1.0 - 0.9 ** 10
SECOND_FIX = 1.0 - 0.99 ** 10

def gelu_pair(pre_act):
    cumulative = 0.5 * (1.0 + jax.scipy.special.erf(pre_act * INV_ROOT2))
    density = jnp.exp(-0.5 * pre_act * pre_act) * INV_ROOT2PI
    return (pre_act * cumulative, cumulative + pre_act * density)

def adam_step(grad, first, second):
    first_new = 0.9 * first + 0.1 * grad
    second_new = 0.99 * second + 0.01 * grad * grad
    step_dir = first_new / FIRST_FIX / (jnp.sqrt(second_new / SECOND_FIX) + 1e-08)
    return (step_dir.astype(jnp.bfloat16), first_new, second_new)

def rounded(value):
    return lax.optimization_barrier(value.astype(jnp.bfloat16)).astype(jnp.float32)

def reference(normed, out_grad, w_in, w_out, first_in, second_in, first_out, second_out):
    block_width = D // N_MX
    normed_blocks = normed.reshape(TOKENS, N_MX, block_width).transpose(1, 0, 2)
    grad_blocks = out_grad.reshape(TOKENS, N_MX, block_width).transpose(1, 0, 2)
    inner_blocks = w_in.reshape(N_MX, block_width, FFW)
    outer_blocks = w_out.reshape(FFW, N_MX, block_width).transpose(1, 0, 2)

    def add_block(totals, block_items):
        normed_b, grad_b, inner_b, outer_b = block_items
        pre_part = rounded(jnp.dot(normed_b, inner_b, preferred_element_type=jnp.float32))
        back_part = rounded(jnp.dot(grad_b, outer_b.T, preferred_element_type=jnp.float32))
        return ((totals[0] + pre_part, totals[1] + back_part), None)
    zeros = jnp.zeros((TOKENS, FFW), jnp.float32)
    (pre_act, act_back), _ = lax.scan(add_block, (zeros, zeros), (normed_blocks, grad_blocks, inner_blocks, outer_blocks))
    value, slope = gelu_pair(pre_act)
    act = value.astype(jnp.bfloat16)
    act_grad = (act_back * slope).astype(jnp.bfloat16)
    grad_out = jnp.dot(act.T, out_grad, preferred_element_type=jnp.float32) / float(IMAGES)
    grad_in = jnp.dot(normed.T, act_grad, preferred_element_type=jnp.float32) / float(IMAGES)
    input_grad = jnp.dot(act_grad, w_in.T, preferred_element_type=jnp.float32).astype(jnp.bfloat16)
    update_in, new_first_in, new_second_in = adam_step(grad_in, first_in, second_in)
    update_out, new_first_out, new_second_out = adam_step(grad_out, first_out, second_out)
    return (input_grad, update_in, new_first_in, new_second_in, update_out, new_first_out, new_second_out)
```

```python
import jax
import jax.numpy as jnp
from jax import lax
from jax.experimental import pallas as pl
from jax.experimental.pallas import tpu as pltpu
from jax.sharding import PartitionSpec as P

PATCHES = 256
NZ = 8
NY = 4
INV_ROOT2 = 0.7071067811865476
INV_ROOT2PI = 0.3989422804014327
FIRST_FIX = 1.0 - 0.9**10
SECOND_FIX = 1.0 - 0.99**10
BF16 = jnp.bfloat16
F32 = jnp.float32
VMEM_BYTES = 48 * 1024 * 1024


def swap_core(value):
    return lax.ppermute(value, "dp", [(i, i ^ 1) for i in range(4)])


def swap_x_lo(value):
    return lax.ppermute(value, "dp", [(i, i ^ 2) for i in range(4)])


def swap_x_hi(value):
    return lax.ppermute(value, "mx", [(i, i ^ 1) for i in range(16)])


def swap_x_both(value):
    pairs = [(d * 16 + m, (d ^ 2) * 16 + (m ^ 1)) for d in range(4) for m in range(16)]
    return lax.ppermute(value, ("dp", "mx"), pairs)


def shift_z(value, by):
    return lax.ppermute(value, "mx", [(i, (i + 2 * by) % 16) for i in range(16)])


def shift_y(value, by):
    return lax.ppermute(value, "my", [(i, (i + by) % NY) for i in range(NY)])


def vmem_specs(count):
    return [pl.BlockSpec(memory_space=pltpu.VMEM)] * count


def call_kernel(kernel, out_shapes, operands, scratch, flops, scalars=None):
    moved = sum(o.size * o.dtype.itemsize for o in operands)
    moved += sum(o.size * o.dtype.itemsize for o in out_shapes)
    in_specs = vmem_specs(len(operands))
    if scalars is not None:
        in_specs = [pl.BlockSpec(memory_space=pltpu.SMEM)] + in_specs
        operands = [scalars] + list(operands)
    return pl.pallas_call(
        kernel,
        out_shape=out_shapes,
        in_specs=in_specs,
        out_specs=vmem_specs(len(out_shapes)),
        scratch_shapes=scratch,
        compiler_params=pltpu.CompilerParams(vmem_limit_bytes=VMEM_BYTES),
        cost_estimate=pl.CostEstimate(flops=flops, bytes_accessed=moved, transcendentals=0),
    )(*operands)


def assemble_tokens(place, own, quarters, whole, rows, width):
    z, y = place[0], place[1]
    for c in range(NY):
        at = pl.multiple_of(lax.rem(c + NZ - z, NZ) * rows, rows)
        whole[pl.ds(at, rows), :width] = own[c * rows : (c + 1) * rows, :]
    for j in range(NY):
        c = lax.rem(y + j, NY)
        near = pl.multiple_of(lax.rem(c + NZ - z, NZ) * rows, rows)
        far = pl.multiple_of(lax.rem(c + NY + NZ - z, NZ) * rows, rows)
        whole[pl.ds(far, rows), :width] = quarters[j][0]
        whole[pl.ds(far, rows), width:] = quarters[j][1]
        whole[pl.ds(near, rows), width:] = quarters[j][2]


def partial_kernel(by_rows, place, own, q0, q1, q2, q3, keep, other, part, part_other, out, whole, weight):
    rows, width = q0.shape[1], q0.shape[2]
    hid = keep.shape[1] if by_rows else keep.shape[0]
    assemble_tokens(place, own, (q0, q1, q2, q3), whole, rows, width)
    if by_rows:
        weight[:width, :hid] = keep[...]
        weight[:width, hid:] = other[...]
        weight[width:, :hid] = part[...]
        weight[width:, hid:] = part_other[...]
    else:
        weight[:hid, :width] = keep[...]
        weight[hid:, :width] = other[...]
        weight[:hid, width:] = part[...]
        weight[hid:, width:] = part_other[...]
    contract = (((1,), (0,)), ((), ())) if by_rows else (((1,), (1,)), ((), ()))
    for k in range(0, NZ, 2):
        rows_k = slice(k * rows, (k + 2) * rows)
        both = lax.dot_general(whole[rows_k, :], weight[...], contract, preferred_element_type=F32)
        out[k] = both[:rows].astype(BF16)
        out[k + 1] = both[rows:].astype(BF16)


def partial_sums(by_rows, place, own, quarters, weights):
    _, rows, width = quarters[0].shape
    hid = weights[0].shape[1 if by_rows else 0]
    outs = [
        jax.ShapeDtypeStruct((NZ, rows, 2 * hid), BF16),
        jax.ShapeDtypeStruct((NZ * rows, 2 * width), BF16),
        jax.ShapeDtypeStruct((2 * width, 2 * hid) if by_rows else (2 * hid, 2 * width), BF16),
    ]
    flops = 2 * NZ * rows * 2 * width * 2 * hid

    def kernel(*refs):
        partial_kernel(by_rows, *refs)

    return call_kernel(kernel, outs, [own, *quarters, *weights], [], flops, place)


def grad_kernel(scale, tokens_left, *refs):
    chunks, tokens, out, whole = refs[:NZ], refs[NZ], refs[NZ + 1], refs[NZ + 2]
    rows = chunks[0].shape[0]
    for k in range(NZ):
        whole[k * rows : (k + 1) * rows, :] = chunks[k][...]
    hid = out.shape[3] if tokens_left else out.shape[2]
    width = out.shape[2] if tokens_left else out.shape[3]
    over = (((0,), (0,)), ((), ()))
    for d in range(2):
        for f in range(2):
            units = whole[:, f * hid : (f + 1) * hid]
            columns = tokens[:, d * width : (d + 1) * width]
            left, right = (columns, units) if tokens_left else (units, columns)
            total = lax.dot_general(left, right, over, preferred_element_type=F32)
            out[f, d] = (total * scale).astype(BF16)


def weight_grad(tokens_left, scale, chunks, tokens):
    rows, hid2 = chunks[0].shape
    width2 = tokens.shape[1]
    hid, width = hid2 // 2, width2 // 2
    tail = (width, hid) if tokens_left else (hid, width)
    outs = [jax.ShapeDtypeStruct((2, 2) + tail, BF16)]
    flops = 2 * NZ * rows * hid2 * width2

    def kernel(*refs):
        grad_kernel(scale, tokens_left, *refs)

    scratch = [pltpu.VMEM((NZ * rows, hid2), BF16)]
    return call_kernel(kernel, outs, [*chunks, tokens], scratch, flops)[0]


def back_kernel(place, *refs):
    chunks, weight, outs, whole = refs[:NZ], refs[NZ], refs[NZ + 1 : NZ + 1 + NY], refs[NZ + 1 + NY]
    z, y = place[0], place[1]
    rows = chunks[0].shape[0]
    width = outs[0].shape[3]
    for k in range(NZ):
        whole[k * rows : (k + 1) * rows, :] = chunks[k][...]
    for j in range(NY):
        c = lax.rem(y + j, NY)
        near = pl.multiple_of(lax.rem(c + NZ - z, NZ) * rows, rows)
        far = pl.multiple_of(lax.rem(c + NY + NZ - z, NZ) * rows, rows)
        for side, at in enumerate((near, far)):
            total = lax.dot_general(
                whole[pl.ds(at, rows), :],
                weight[...],
                (((1,), (1,)), ((), ())),
                preferred_element_type=F32,
            )
            outs[j][side, 0] = total[:, :width].astype(BF16)
            outs[j][side, 1] = total[:, width:].astype(BF16)


def token_grad(place, chunks, weight):
    rows, hid2 = chunks[0].shape
    width2 = weight.shape[0]
    outs = [jax.ShapeDtypeStruct((2, 2, rows, width2 // 2), BF16)] * NY
    flops = 2 * NZ * rows * hid2 * width2
    scratch = [pltpu.VMEM((NZ * rows, hid2), BF16)]
    return call_kernel(back_kernel, outs, [*chunks, weight], scratch, flops, place)


def gelu_pair(pre_act):
    cumulative = 0.5 * (1.0 + jax.scipy.special.erf(pre_act * INV_ROOT2))
    density = jnp.exp(-0.5 * pre_act * pre_act) * INV_ROOT2PI
    return (pre_act * cumulative, cumulative + pre_act * density)


def adam_step(grad, first, second):
    first_new = 0.9 * first + 0.1 * grad
    second_new = 0.99 * second + 0.01 * grad * grad
    step_dir = first_new / FIRST_FIX / (jnp.sqrt(second_new / SECOND_FIX) + 1e-08)
    return (step_dir.astype(BF16), first_new, second_new)


def add_rounded(moving, mine):
    return (moving.astype(F32) + mine.astype(F32)).astype(BF16)


def reduce_over_z(parts, long_way):
    far = parts[4]
    order = (5, 6, 7) if long_way < 0 else (3, 2, 1)
    for k in order:
        far = add_rounded(shift_z(far, long_way), parts[k])
    far = shift_z(far, long_way)
    order = (3, 2, 1) if long_way < 0 else (5, 6, 7)
    near = parts[order[0]]
    for k in order[1:]:
        near = add_rounded(shift_z(near, -long_way), parts[k])
    near = shift_z(near, -long_way)
    return parts[0].astype(F32) + far.astype(F32) + near.astype(F32)


def gather_over_z(chunk, long_way):
    found = [chunk] + [None] * (NZ - 1)
    far = near = chunk
    for step in range(1, 5):
        far = shift_z(far, long_way)
        found[(-long_way * step) % NZ] = far
        if step < 4:
            near = shift_z(near, -long_way)
            found[(long_way * step) % NZ] = near
    return found


def halves(value, axis, which):
    size = value.shape[axis] // 2
    return (
        lax.dynamic_slice_in_dim(value, which * size, size, axis),
        lax.dynamic_slice_in_dim(value, (1 - which) * size, size, axis),
    )


def share_of_grad(partial, axis, x_hi):
    moved = swap_core(partial[1])
    there = swap_x_hi(add_rounded(moved[1], partial[0, 1]))
    here = partial[0, 0].astype(F32) + moved[0].astype(F32)
    there = there.astype(F32)
    return jnp.where(
        x_hi == 0,
        jnp.concatenate([here, there], axis=axis),
        jnp.concatenate([there, here], axis=axis),
    )


def body(normed, out_grad, w_in, w_out, first_in, second_in, first_out, second_out):
    mx = lax.axis_index("mx")
    y = lax.axis_index("my")
    z, x_hi = mx // 2, mx % 2
    place = jnp.stack([z, y]).astype(jnp.int32)
    rows = normed.shape[0] // NY

    def spread(array):
        quarter = lax.dynamic_slice_in_dim(array, y * rows, rows, 0)
        mine = jnp.stack([swap_x_lo(quarter), swap_x_both(quarter), swap_x_hi(quarter)])
        return [mine, shift_y(mine, -1), shift_y(mine, 2), shift_y(mine, 1)]

    def weights(array, axis):
        keep, send = halves(array, axis, x_hi)
        part = swap_x_hi(send)
        return [keep, swap_core(keep), part, swap_core(part)]

    tokens_in = spread(normed)
    weights_in = weights(w_in, 1)
    tokens_out = spread(out_grad)
    weights_out = weights(w_out, 0)
    pre_parts, whole_in, weight_in = partial_sums(True, place, normed, tokens_in, weights_in)
    back_parts, whole_out, _ = partial_sums(False, place, out_grad, tokens_out, weights_out)
    pre_act = reduce_over_z(pre_parts, -1)
    act_back = reduce_over_z(back_parts, 1)
    value, slope = gelu_pair(pre_act)
    act = gather_over_z(value.astype(BF16), 1)
    act_grad = gather_over_z((act_back * slope).astype(BF16), -1)
    images = float(normed.shape[0] * lax.axis_size("dp") // PATCHES)
    partial_out = weight_grad(False, 1.0 / images, act, whole_out)
    outs = token_grad(place, act_grad, weight_in)
    partial_in = weight_grad(True, 1.0 / images, act_grad, whole_in)
    share_out = share_of_grad(partial_out, 0, x_hi)
    share_in = share_of_grad(partial_in, 1, x_hi)
    moved = [shift_y(outs[1], 1), shift_y(outs[2], 2), shift_y(outs[3], 3)]
    total = sum((m.astype(F32) for m in moved), outs[0].astype(F32))
    rounded = total.astype(BF16)
    input_grad = (
        total[0, 0]
        + swap_x_lo(rounded[1, 0]).astype(F32)
        + swap_x_hi(rounded[0, 1]).astype(F32)
        + swap_x_both(rounded[1, 1]).astype(F32)
    ).astype(BF16)
    update_out, new_first_out, new_second_out = adam_step(share_out, first_out, second_out)
    update_in, new_first_in, new_second_in = adam_step(share_in, first_in, second_in)
    return (
        input_grad,
        update_in,
        new_first_in,
        new_second_in,
        update_out,
        new_first_out,
        new_second_out,
    )


def solution(mesh):
    in_specs = (
        P("dp", "mx"),
        P("dp", "mx"),
        P("mx", ("my", "dp")),
        P(("my", "dp"), "mx"),
        P("mx", ("my", "dp")),
        P("mx", ("my", "dp")),
        P(("my", "dp"), "mx"),
        P(("my", "dp"), "mx"),
    )
    out_specs = (
        P(("dp", "my"), "mx"),
        P("mx", ("my", "dp")),
        P("mx", ("my", "dp")),
        P("mx", ("my", "dp")),
        P(("my", "dp"), "mx"),
        P(("my", "dp"), "mx"),
        P(("my", "dp"), "mx"),
    )
    return jax.shard_map(body, mesh=mesh, in_specs=in_specs, out_specs=out_specs, check_vma=False)
```

```python
import functools

import jax
import jax.numpy as jnp
from jax import lax
from jax.experimental import pallas as pl
from jax.experimental.pallas import tpu as pltpu
from jax.sharding import PartitionSpec as P

PATCHES = 256
NZ = 8
NY = 4
INV_ROOT2 = 0.7071067811865476
INV_ROOT2PI = 0.3989422804014327
FIRST_FIX = 1.0 - 0.9**10
SECOND_FIX = 1.0 - 0.99**10
BF16 = jnp.bfloat16
F32 = jnp.float32
VMEM_BYTES = 48 * 1024 * 1024


def swap_core(value):
    return lax.ppermute(value, "dp", [(i, i ^ 1) for i in range(4)])


def swap_x_lo(value):
    return lax.ppermute(value, "dp", [(i, i ^ 2) for i in range(4)])


def swap_x_hi(value):
    return lax.ppermute(value, "mx", [(i, i ^ 1) for i in range(16)])


def swap_x_both(value):
    pairs = [(d * 16 + m, (d ^ 2) * 16 + (m ^ 1)) for d in range(4) for m in range(16)]
    return lax.ppermute(value, ("dp", "mx"), pairs)


def shift_z(value, by):
    return lax.ppermute(value, "mx", [(i, (i + 2 * by) % 16) for i in range(16)])


def shift_y(value, by):
    return lax.ppermute(value, "my", [(i, (i + by) % NY) for i in range(NY)])


def vmem_specs(count):
    return [pl.BlockSpec(memory_space=pltpu.VMEM)] * count


def call_kernel(kernel, out_shapes, operands, scratch=(), flops=0, scalars=None, follows=()):
    operands, follows = list(operands), list(follows)
    moved = sum(o.size * o.dtype.itemsize for o in operands)
    moved += sum(o.size * o.dtype.itemsize for o in out_shapes)
    in_specs = vmem_specs(len(operands))
    in_specs += [pl.BlockSpec(memory_space=pl.ANY)] * len(follows)
    skip, count = len(operands), len(follows)
    operands += follows
    if scalars is not None:
        in_specs = [pl.BlockSpec(memory_space=pltpu.SMEM)] + in_specs
        operands = [scalars] + operands
        skip += 1

    def run(*refs):
        kernel(*refs[:skip], *refs[skip + count :])

    return pl.pallas_call(
        run,
        out_shape=out_shapes,
        in_specs=in_specs,
        out_specs=vmem_specs(len(out_shapes)),
        scratch_shapes=list(scratch),
        compiler_params=pltpu.CompilerParams(vmem_limit_bytes=VMEM_BYTES),
        cost_estimate=pl.CostEstimate(flops=flops, bytes_accessed=moved, transcendentals=0),
    )(*operands)


def like(array, shape=None, dtype=None):
    return jax.ShapeDtypeStruct(shape or array.shape, dtype or array.dtype)


def split_first(axis, place, tokens, weight, quarter, keep, send):
    y, x_hi = place[1], place[2]
    rows = quarter.shape[0]
    quarter[...] = tokens[pl.ds(pl.multiple_of(y * rows, rows), rows), :]
    split_weight(axis, x_hi, weight, keep, send)


def split_weight(axis, x_hi, weight, keep, send):
    size = weight.shape[axis] // 2
    for out, which in ((keep, x_hi), (send, 1 - x_hi)):
        half = pl.ds(pl.multiple_of(which * size, size), size)
        out[...] = weight[half, :] if axis == 0 else weight[:, half]


def split_later(axis, place, tokens, weight, copied, quarter, keep, send):
    copied[...] = tokens[...]
    split_first(axis, place, tokens, weight, quarter, keep, send)


def stack_kernel(one, two, three, out):
    out[0] = one[...]
    out[1] = two[...]
    out[2] = three[...]


def add_kernel(moving, mine, out):
    out[...] = (moving[...].astype(F32) + mine[...].astype(F32)).astype(BF16)


def add_rounded(moving, mine, follows=()):
    return call_kernel(add_kernel, [like(mine)], [moving, mine], follows=follows)[0]


def act_kernel(own, far, near, act, slope):
    pre_act = own[...].astype(F32) + far[...].astype(F32) + near[...].astype(F32)
    value, slope[...] = gelu_pair(pre_act)
    act[...] = value.astype(BF16)


def act_grad_kernel(own, far, near, slope, out):
    act_back = own[...].astype(F32) + far[...].astype(F32) + near[...].astype(F32)
    out[...] = (act_back * slope[...]).astype(BF16)


def assemble_tokens(place, own, moved, whole, rows, width):
    z, y = place[0], place[1]
    step = rows // NZ

    def put(c, side, yy, right, block):
        k = lax.rem(c + NZ - z, NZ)
        at = pl.multiple_of(((k * 2 + side) * NY + yy) * step, step)
        columns = slice(width, 2 * width) if right else slice(0, width)
        whole[pl.ds(at, step), columns] = block

    for c in range(NZ):
        for yy in range(NY):
            line = slice(yy * rows + c * step, yy * rows + (c + 1) * step)
            put(c, 0, yy, False, own[line, :])
            if len(moved) > NY:
                put(c, 1, yy, False, moved[NY][line, :])
                put(c, 1, yy, True, moved[NY + 1][line, :])
        line = slice(c * step, (c + 1) * step)
        for j in range(NY):
            yy = lax.rem(y + j, NY)
            if len(moved) > NY:
                put(c, 0, yy, True, moved[j][line, :])
            else:
                put(c, 1, yy, False, moved[j][0, line, :])
                put(c, 1, yy, True, moved[j][1, line, :])
                put(c, 0, yy, True, moved[j][2, line, :])


def partial_kernel(by_rows, place, own, *refs):
    moved, (keep, other, part, part_other) = refs[: -NZ - 6], refs[-NZ - 6 : -NZ - 2]
    out, (whole, weight) = refs[-NZ - 2 : -2], refs[-2:]
    rows, width = own.shape[0] // NY, own.shape[1]
    hid = keep.shape[1] if by_rows else keep.shape[0]
    assemble_tokens(place, own, moved, whole, rows, width)
    if by_rows:
        weight[:width, :hid] = keep[...]
        weight[:width, hid:] = other[...]
        weight[width:, :hid] = part[...]
        weight[width:, hid:] = part_other[...]
    else:
        weight[:hid, :width] = keep[...]
        weight[hid:, :width] = other[...]
        weight[:hid, width:] = part[...]
        weight[hid:, width:] = part_other[...]
    contract = (((1,), (0,)), ((), ())) if by_rows else (((1,), (1,)), ((), ()))
    for k in range(0, NZ, 2):
        rows_k = slice(k * rows, (k + 2) * rows)
        both = lax.dot_general(whole[rows_k, :], weight[...], contract, preferred_element_type=F32)
        out[k][...] = both[:rows].astype(BF16)
        out[k + 1][...] = both[rows:].astype(BF16)


def partial_sums(by_rows, place, own, moved, weights, follows=()):
    rows, width = own.shape[0] // NY, own.shape[1]
    hid = weights[0].shape[1 if by_rows else 0]
    outs = [jax.ShapeDtypeStruct((rows, 2 * hid), BF16)] * NZ + [
        jax.ShapeDtypeStruct((NZ * rows, 2 * width), BF16),
        jax.ShapeDtypeStruct((2 * width, 2 * hid) if by_rows else (2 * hid, 2 * width), BF16),
    ]
    flops = 2 * NZ * rows * 2 * width * 2 * hid

    def kernel(*refs):
        partial_kernel(by_rows, *refs)

    results = call_kernel(kernel, outs, [own, *moved, *weights], [], flops, place, follows)
    return results[:NZ], results[NZ], results[NZ + 1]


def grad_kernel(scale, tokens_left, *refs):
    chunks, tokens, outs, whole = refs[:NZ], refs[NZ], refs[NZ + 1 : NZ + 3], refs[NZ + 3]
    rows = chunks[0].shape[0]
    for k in range(NZ):
        whole[k * rows : (k + 1) * rows, :] = chunks[k][...]
    width, hid = outs[0].shape[1:] if tokens_left else outs[0].shape[:0:-1]
    over = (((0,), (0,)), ((), ()))
    for d in range(2):
        for f in range(2):
            units = whole[:, f * hid : (f + 1) * hid]
            columns = tokens[:, d * width : (d + 1) * width]
            left, right = (columns, units) if tokens_left else (units, columns)
            total = lax.dot_general(left, right, over, preferred_element_type=F32)
            outs[f][d] = (total * scale).astype(BF16)


def weight_grad(tokens_left, scale, chunks, tokens, follows=()):
    rows, hid2 = chunks[0].shape
    width2 = tokens.shape[1]
    hid, width = hid2 // 2, width2 // 2
    tail = (width, hid) if tokens_left else (hid, width)
    outs = [jax.ShapeDtypeStruct((2,) + tail, BF16)] * 2
    flops = 2 * NZ * rows * hid2 * width2

    def kernel(*refs):
        grad_kernel(scale, tokens_left, *refs)

    scratch = [pltpu.VMEM((NZ * rows, hid2), BF16)]
    return call_kernel(kernel, outs, [*chunks, tokens], scratch, flops, follows=follows)


def back_kernel(count, place, *refs):
    chunks, weight = refs[:count], refs[count]
    outs, whole, total = refs[count + 1 : count + 1 + NY], refs[-2], refs[-1]
    y = place[1]
    rows = chunks[0].shape[0]
    step = rows // NZ
    width = outs[0].shape[3]
    for k in range(count):
        whole[k * rows : (k + 1) * rows, :] = chunks[k][...]
    total[...] = lax.dot_general(
        whole[...], weight[...], (((1,), (1,)), ((), ())), preferred_element_type=F32
    ).astype(BF16)
    for j in range(NY):
        yy = lax.rem(y + j, NY)
        for k in range(count):
            for side in range(2):
                at = pl.multiple_of(((k * 2 + side) * NY + yy) * step, step)
                line = slice(k * step, (k + 1) * step)
                for d in range(2):
                    columns = slice(d * width, (d + 1) * width)
                    outs[j][side, d, line, :] = total[pl.ds(at, step), columns]


def token_grad(place, chunks, weight, follows=()):
    count = len(chunks)
    rows, hid2 = chunks[0].shape
    width2 = weight.shape[0]
    outs = [jax.ShapeDtypeStruct((2, 2, count * rows // NZ, width2 // 2), BF16)] * NY
    flops = 2 * count * rows * hid2 * width2
    scratch = [pltpu.VMEM((count * rows, hid2), BF16), pltpu.VMEM((count * rows, width2), BF16)]

    def kernel(*refs):
        back_kernel(count, *refs)

    return call_kernel(kernel, outs, [*chunks, weight], scratch, flops, place, follows)


def send_over_y(outs):
    return [outs[0], shift_y(outs[1], 1), shift_y(outs[2], 2), shift_y(outs[3], 3)]


def sum_kernel(*refs):
    terms, outs = refs[:-4], refs[-4:]
    at = 0
    for group in (terms[:NY], terms[NY:]):
        size = group[0].shape[2]
        for side in range(2):
            for d in range(2):
                total = sum(term[side, d].astype(F32) for term in group)
                out = outs[side * 2 + d]
                out[at : at + size, :] = total.astype(out.dtype)
        at += size


def place_kernel(order, place, own, one, two, three, out):
    z = place[0]
    step = out.shape[0] // NZ
    for i, k in enumerate(order):
        line = slice(i * step, (i + 1) * step)
        total = own[line, :] + one[line, :].astype(F32)
        total += two[line, :].astype(F32) + three[line, :].astype(F32)
        at = pl.multiple_of(lax.rem(z + k, NZ) * step, step)
        out[pl.ds(at, step), :] = total.astype(BF16)


def gelu_pair(pre_act):
    cumulative = 0.5 * (1.0 + jax.scipy.special.erf(pre_act * INV_ROOT2))
    density = jnp.exp(-0.5 * pre_act * pre_act) * INV_ROOT2PI
    return (pre_act * cumulative, cumulative + pre_act * density)


def adam_step(grad, first, second):
    first_new = 0.9 * first + 0.1 * grad
    second_new = 0.99 * second + 0.01 * grad * grad
    step_dir = first_new / FIRST_FIX / (jnp.sqrt(second_new / SECOND_FIX) + 1e-08)
    return (step_dir.astype(BF16), first_new, second_new)


def reduce_over_z(parts, long_way, follows=()):
    far = parts[4]
    order = (5, 6, 7) if long_way < 0 else (3, 2, 1)
    for k in order:
        far = add_rounded(shift_z(far, long_way), parts[k], follows)
    far = shift_z(far, long_way)
    order = (3, 2, 1) if long_way < 0 else (5, 6, 7)
    near = parts[order[0]]
    for k in order[1:]:
        near = add_rounded(shift_z(near, -long_way), parts[k])
    near = shift_z(near, -long_way)
    return parts[0], far, near


def gather_over_z(chunk, long_way):
    found = [chunk] + [None] * (NZ - 1)
    far = near = chunk
    for step in range(1, 5):
        far = shift_z(far, long_way)
        found[(-long_way * step) % NZ] = far
        if step < 4:
            near = shift_z(near, -long_way)
            found[(long_way * step) % NZ] = near
    return found


def share_of_grad(partial, axis, x_hi):
    kept, sent = partial
    moved = swap_core(sent)
    leaving = (moved[1].astype(F32) + kept[1].astype(F32)).astype(BF16)
    there = swap_x_hi(leaving)
    here = kept[0].astype(F32) + moved[0].astype(F32)
    wide = there.astype(F32)
    share = jnp.where(
        x_hi == 0,
        jnp.concatenate([here, wide], axis=axis),
        jnp.concatenate([wide, here], axis=axis),
    )
    return share, leaving


def body(normed, out_grad, w_in, w_out, first_in, second_in, first_out, second_out):
    mx = lax.axis_index("mx")
    y = lax.axis_index("my")
    z, x_hi = mx // 2, mx % 2
    place = jnp.stack([z, y, x_hi]).astype(jnp.int32)
    rows = normed.shape[0] // NY
    width, hid = w_in.shape[0], w_in.shape[1] // 2

    quarter, keep_in, send_in = call_kernel(
        functools.partial(split_first, 1),
        [like(normed, (rows, width)), like(w_in, (width, hid)), like(w_in, (width, hid))],
        [normed, w_in],
        scalars=place,
    )
    quarters = [swap_x_lo(quarter), swap_x_both(quarter), swap_x_hi(quarter)]
    part_in = swap_x_hi(send_in)
    other_in = swap_core(keep_in)
    mine = call_kernel(
        stack_kernel, [like(normed, (3, rows, width))], quarters, follows=[other_in]
    )[0]
    tokens_in = [mine, shift_y(mine, -1), shift_y(mine, 2), shift_y(mine, 1)]
    weights_in = [keep_in, other_in, part_in, swap_core(part_in)]
    sent, quarter_out, keep_out, send_out = call_kernel(
        functools.partial(split_later, 0),
        [like(out_grad), like(quarter)] + [like(w_out, (hid, width))] * 2,
        [out_grad, w_out],
        scalars=place,
        follows=[mine, part_in],
    )
    across = swap_x_hi(quarter_out)
    beside = [swap_x_lo(sent), swap_x_both(sent)]
    other_out = swap_core(keep_out)
    pre_parts, whole_in, weight_in = partial_sums(
        True, place, normed, tokens_in, weights_in, [across, other_out]
    )
    tokens_out = [across, shift_y(across, -1), shift_y(across, 2), shift_y(across, 1)] + beside
    part_out = swap_x_hi(send_out)
    weights_out = [keep_out, other_out, part_out, swap_core(part_out)]
    back_parts, whole_out, _ = partial_sums(
        False, place, out_grad, tokens_out, weights_out, [pre_parts[4]]
    )
    pre_terms = reduce_over_z(pre_parts, -1, beside)
    chunk = pre_parts[0]
    act, slope = call_kernel(act_kernel, [like(chunk), like(chunk, dtype=F32)], pre_terms)
    acts = gather_over_z(act, 1)
    back_terms = reduce_over_z(back_parts, 1)
    act_grad = call_kernel(act_grad_kernel, [like(chunk)], [*back_terms, slope])[0]
    act_grads = gather_over_z(act_grad, -1)

    images = float(normed.shape[0] * lax.axis_size("dp") // PATCHES)
    partial_out = weight_grad(False, 1.0 / images, acts, whole_out)
    share_out, leaving_out = share_of_grad(partial_out, 0, x_hi)
    first_places, last_places = (0, 1, 7, 2, 6), (3, 5, 4)
    early = token_grad(place, [act_grads[k] for k in first_places], weight_in)
    moved = send_over_y(early)
    late = token_grad(place, [act_grads[k] for k in last_places], weight_in, [leaving_out])
    partial_in = weight_grad(True, 1.0 / images, act_grads, whole_in, moved[1:NY])
    moved += send_over_y(late)
    share_in, _ = share_of_grad(partial_in, 1, x_hi)
    block = (rows, width)
    own, part, other, both = call_kernel(
        sum_kernel, [like(normed, block, F32)] + [like(normed, block)] * 3, moved
    )
    input_grad = call_kernel(
        functools.partial(place_kernel, first_places + last_places),
        [like(normed, block)],
        [own, swap_x_lo(other), swap_x_hi(part), swap_x_both(both)],
        scalars=place,
    )[0]
    update_out, new_first_out, new_second_out = adam_step(share_out, first_out, second_out)
    update_in, new_first_in, new_second_in = adam_step(share_in, first_in, second_in)
    return (
        input_grad,
        update_in,
        new_first_in,
        new_second_in,
        update_out,
        new_first_out,
        new_second_out,
    )


def solution(mesh):
    in_specs = (
        P("dp", "mx"),
        P("dp", "mx"),
        P("mx", ("my", "dp")),
        P(("my", "dp"), "mx"),
        P("mx", ("my", "dp")),
        P("mx", ("my", "dp")),
        P(("my", "dp"), "mx"),
        P(("my", "dp"), "mx"),
    )
    out_specs = (
        P(("dp", "my"), "mx"),
        P("mx", ("my", "dp")),
        P("mx", ("my", "dp")),
        P("mx", ("my", "dp")),
        P(("my", "dp"), "mx"),
        P(("my", "dp"), "mx"),
        P(("my", "dp"), "mx"),
    )
    return jax.shard_map(body, mesh=mesh, in_specs=in_specs, out_specs=out_specs, check_vma=False)
```

```python
import functools

import jax
import jax.numpy as jnp
from jax import lax
from jax.experimental import pallas as pl
from jax.experimental.pallas import tpu as pltpu
from jax.sharding import PartitionSpec as P

PATCHES = 256
NZ = 8
NY = 4
INV_ROOT2 = 0.7071067811865476
INV_ROOT2PI = 0.3989422804014327
FIRST_FIX = 1.0 - 0.9**10
SECOND_FIX = 1.0 - 0.99**10
BF16 = jnp.bfloat16
F32 = jnp.float32
VMEM_BYTES = 24 * 1024 * 1024
WHOLE_VMEM_BYTES = 63 * 1024 * 1024


def swap_core(value):
    return lax.ppermute(value, "dp", [(i, i ^ 1) for i in range(4)])


def swap_x_lo(value):
    return lax.ppermute(value, "dp", [(i, i ^ 2) for i in range(4)])


def swap_x_hi(value):
    return lax.ppermute(value, "mx", [(i, i ^ 1) for i in range(16)])


def swap_x_both(value):
    pairs = [(d * 16 + m, (d ^ 2) * 16 + (m ^ 1)) for d in range(4) for m in range(16)]
    return lax.ppermute(value, ("dp", "mx"), pairs)


def shift_z(value, by):
    return lax.ppermute(value, "mx", [(i, (i + 2 * by) % 16) for i in range(16)])


def shift_y(value, by):
    return lax.ppermute(value, "my", [(i, (i + by) % NY) for i in range(NY)])


def vmem_specs(count):
    return [pl.BlockSpec(memory_space=pltpu.VMEM)] * count


def call_kernel(kernel, out_shapes, operands, scratch=(), flops=0, scalars=None, follows=()):
    operands, follows = list(operands), list(follows)
    moved = sum(o.size * o.dtype.itemsize for o in operands)
    moved += sum(o.size * o.dtype.itemsize for o in out_shapes)
    in_specs = vmem_specs(len(operands))
    in_specs += [pl.BlockSpec(memory_space=pl.ANY)] * len(follows)
    skip, count = len(operands), len(follows)
    operands += follows
    if scalars is not None:
        in_specs = [pl.BlockSpec(memory_space=pltpu.SMEM)] + in_specs
        operands = [scalars] + operands
        skip += 1

    def run(*refs):
        kernel(*refs[:skip], *refs[skip + count :])

    return pl.pallas_call(
        run,
        out_shape=out_shapes,
        in_specs=in_specs,
        out_specs=vmem_specs(len(out_shapes)),
        scratch_shapes=list(scratch),
        compiler_params=pltpu.CompilerParams(vmem_limit_bytes=VMEM_BYTES),
        cost_estimate=pl.CostEstimate(flops=0, bytes_accessed=0, transcendentals=0),
    )(*operands)


def like(array, shape=None, dtype=None):
    return jax.ShapeDtypeStruct(shape or array.shape, dtype or array.dtype)


def copy_all(pairs, sems):
    copies = [pltpu.make_async_copy(src, dst, sems.at[i]) for i, (src, dst) in enumerate(pairs)]
    for copy in copies:
        copy.start()
    for copy in copies:
        copy.wait()


def copy_kernel(kernel, out_shapes, place, operands, copies):
    return pl.pallas_call(
        kernel,
        out_shape=out_shapes,
        in_specs=[pl.BlockSpec(memory_space=pltpu.SMEM)]
        + [pl.BlockSpec(memory_space=pltpu.HBM)] * len(operands),
        out_specs=vmem_specs(len(out_shapes)),
        scratch_shapes=[pltpu.SemaphoreType.DMA((copies,))],
        compiler_params=pltpu.CompilerParams(vmem_limit_bytes=WHOLE_VMEM_BYTES),
        cost_estimate=pl.CostEstimate(flops=0, bytes_accessed=0, transcendentals=0),
    )(place, *operands)


def split_kernel(
    place, tokens, cotangent, w_in, w_out, alone, pair, keep, send, copied, sems
):
    rows, size = alone.shape[0], keep.shape[1]
    line = pl.ds(pl.multiple_of(place[1] * rows, rows), rows)
    mine = tokens.at[line, :]
    pairs = [(mine, alone), (mine, pair.at[0]), (cotangent.at[line, :], pair.at[1])]
    for out, which in ((keep, place[2]), (send, 1 - place[2])):
        half = pl.ds(pl.multiple_of(which * size, size), size)
        pairs += [(w_in.at[:, half], out.at[0]), (w_out.at[half, :], out.at[1])]
    pairs.append((cotangent, copied))
    copy_all(pairs, sems)


def pass_kernel(one, two, out_one, out_two):
    out_one[...] = one[...]
    out_two[...] = two[...]


def forward_kernel(before, beyond, up, down):
    size = up.shape[0]
    up[...] = before[:size]
    down[...] = beyond[size:]


def stack_kernel(one, two, pair, out):
    out[0] = one[...]
    out[1] = two[...]
    out[2] = pair[0]
    out[3] = pair[1]


def add_kernel(moving, mine, out):
    out[...] = (moving[...].astype(F32) + mine[...].astype(F32)).astype(BF16)


def add_rounded(moving, mine, follows=()):
    return call_kernel(add_kernel, [like(mine)], [moving, mine], follows=follows)[0]


def act_kernel(own, far, near, act, slope):
    pre_act = own[...].astype(F32) + far[...].astype(F32) + near[...].astype(F32)
    value, slope[...] = gelu_pair(pre_act)
    act[...] = value.astype(BF16)


def act_grad_kernel(own, far, near, slope, out):
    act_back = own[...].astype(F32) + far[...].astype(F32) + near[...].astype(F32)
    out[...] = (act_back * slope[...]).astype(BF16)


def assemble_tokens(place, own, moved, whole, rows, width):
    z, y = place[0], place[1]
    step = rows // NZ

    def put(c, side, yy, right, block):
        k = lax.rem(c + NZ - z, NZ)
        at = pl.multiple_of(((k * 2 + side) * NY + yy) * step, step)
        columns = slice(width, 2 * width) if right else slice(0, width)
        whole[pl.ds(at, step), columns] = block

    beside = moved[NY + 1 :]

    def piece(j, p, line):
        if j == 2:
            half = moved[2].shape[0]
            return moved[2][p, line, :] if p < half else moved[3][p - half, line, :]
        return moved[j + 1 if j > 2 else j][p, line, :]

    for c in range(NZ):
        for yy in range(NY):
            line = slice(yy * rows + c * step, yy * rows + (c + 1) * step)
            put(c, 0, yy, False, own[line, :])
            if beside:
                put(c, 1, yy, False, beside[0][line, :])
                put(c, 1, yy, True, beside[1][line, :])
        line = slice(c * step, (c + 1) * step)
        for j in range(NY):
            yy = lax.rem(y + j, NY)
            if beside:
                put(c, 0, yy, True, piece(j, 3, line))
            else:
                put(c, 1, yy, False, piece(j, 0, line))
                put(c, 1, yy, True, piece(j, 1, line))
                put(c, 0, yy, True, piece(j, 2, line))


def partial_kernel(by_rows, place, own, *refs):
    moved, (keep, other, part, part_other) = refs[: -NZ - 6], refs[-NZ - 6 : -NZ - 2]
    which = 0 if by_rows else 1
    keep, other, part, part_other = (w.at[which] for w in (keep, other, part, part_other))
    out, (whole, weight) = refs[-NZ - 2 : -2], refs[-2:]
    rows, width = own.shape[0] // NY, own.shape[1]
    hid = keep.shape[1] if by_rows else keep.shape[0]
    assemble_tokens(place, own, moved, whole, rows, width)
    if by_rows:
        weight[:width, :hid] = keep[...]
        weight[:width, hid:] = other[...]
        weight[width:, :hid] = part[...]
        weight[width:, hid:] = part_other[...]
    else:
        weight[:hid, :width] = keep[...]
        weight[hid:, :width] = other[...]
        weight[:hid, width:] = part[...]
        weight[hid:, width:] = part_other[...]
    contract = (((1,), (0,)), ((), ())) if by_rows else (((1,), (1,)), ((), ()))
    for k in range(0, NZ, 2):
        rows_k = slice(k * rows, (k + 2) * rows)
        both = lax.dot_general(whole[rows_k, :], weight[...], contract, preferred_element_type=F32)
        out[k][...] = both[:rows].astype(BF16)
        out[k + 1][...] = both[rows:].astype(BF16)


def partial_sums(by_rows, place, own, moved, weights, follows=()):
    rows, width = own.shape[0] // NY, own.shape[1]
    hid = weights[0].shape[2 if by_rows else 1]
    outs = [jax.ShapeDtypeStruct((rows, 2 * hid), BF16)] * NZ + [
        jax.ShapeDtypeStruct((NZ * rows, 2 * width), BF16),
        jax.ShapeDtypeStruct((2 * width, 2 * hid) if by_rows else (2 * hid, 2 * width), BF16),
    ]
    flops = 2 * NZ * rows * 2 * width * 2 * hid

    def kernel(*refs):
        partial_kernel(by_rows, *refs)

    results = call_kernel(kernel, outs, [own, *moved, *weights], [], flops, place, follows)
    return results[:NZ], results[NZ], results[NZ + 1]


def grad_kernel(scale, tokens_left, *refs):
    chunks, tokens, outs, whole = refs[:NZ], refs[NZ], refs[NZ + 1 : NZ + 3], refs[NZ + 3]
    rows = chunks[0].shape[0]
    for k in range(NZ):
        whole[k * rows : (k + 1) * rows, :] = chunks[k][...]
    width, hid = outs[0].shape[1:] if tokens_left else outs[0].shape[:0:-1]
    over = (((0,), (0,)), ((), ()))
    for d in range(2):
        for f in range(2):
            units = whole[:, f * hid : (f + 1) * hid]
            columns = tokens[:, d * width : (d + 1) * width]
            left, right = (columns, units) if tokens_left else (units, columns)
            total = lax.dot_general(left, right, over, preferred_element_type=F32)
            outs[f][d] = (total * scale).astype(BF16)


def weight_grad(tokens_left, scale, chunks, tokens, follows=()):
    rows, hid2 = chunks[0].shape
    width2 = tokens.shape[1]
    hid, width = hid2 // 2, width2 // 2
    tail = (width, hid) if tokens_left else (hid, width)
    outs = [jax.ShapeDtypeStruct((2,) + tail, BF16)] * 2
    flops = 2 * NZ * rows * hid2 * width2

    def kernel(*refs):
        grad_kernel(scale, tokens_left, *refs)

    scratch = [pltpu.VMEM((NZ * rows, hid2), BF16)]
    return call_kernel(kernel, outs, [*chunks, tokens], scratch, flops, follows=follows)


def back_kernel(count, place, *refs):
    chunks, weight = refs[:count], refs[count]
    outs, whole, total = refs[count + 1 : count + 1 + NY], refs[-2], refs[-1]
    y = place[1]
    rows = chunks[0].shape[0]
    step = rows // NZ
    width = outs[0].shape[3]
    for k in range(count):
        whole[k * rows : (k + 1) * rows, :] = chunks[k][...]
    total[...] = lax.dot_general(
        whole[...], weight[...], (((1,), (1,)), ((), ())), preferred_element_type=F32
    ).astype(BF16)
    for j in range(NY):
        yy = lax.rem(y + j, NY)
        for k in range(count):
            for side in range(2):
                at = pl.multiple_of(((k * 2 + side) * NY + yy) * step, step)
                line = slice(k * step, (k + 1) * step)
                for d in range(2):
                    columns = slice(d * width, (d + 1) * width)
                    outs[j][side, d, line, :] = total[pl.ds(at, step), columns]


def token_grad(place, chunks, weight, follows=()):
    count = len(chunks)
    rows, hid2 = chunks[0].shape
    width2 = weight.shape[0]
    outs = [jax.ShapeDtypeStruct((2, 2, count * rows // NZ, width2 // 2), BF16)] * NY
    flops = 2 * count * rows * hid2 * width2
    scratch = [pltpu.VMEM((count * rows, hid2), BF16), pltpu.VMEM((count * rows, width2), BF16)]

    def kernel(*refs):
        back_kernel(count, *refs)

    return call_kernel(kernel, outs, [*chunks, weight], scratch, flops, place, follows)


def send_over_y(outs):
    return [outs[0], shift_y(outs[1], 1), shift_y(outs[2], 2), shift_y(outs[3], 3)]


def sum_kernel(*refs):
    terms, outs = refs[:-4], refs[-4:]
    at = 0
    for group in (terms[:NY], terms[NY:]):
        size = group[0].shape[2]
        for side in range(2):
            for d in range(2):
                total = sum(term[side, d].astype(F32) for term in group)
                out = outs[side * 2 + d]
                out[at : at + size, :] = total.astype(out.dtype)
        at += size


def place_kernel(order, place, own, one, two, three, out):
    z = place[0]
    step = out.shape[0] // NZ
    for i, k in enumerate(order):
        line = slice(i * step, (i + 1) * step)
        total = own[line, :] + one[line, :].astype(F32)
        total += two[line, :].astype(F32) + three[line, :].astype(F32)
        at = pl.multiple_of(lax.rem(z + k, NZ) * step, step)
        out[pl.ds(at, step), :] = total.astype(BF16)


def gelu_pair(pre_act):
    cumulative = 0.5 * (1.0 + jax.scipy.special.erf(pre_act * INV_ROOT2))
    density = jnp.exp(-0.5 * pre_act * pre_act) * INV_ROOT2PI
    return (pre_act * cumulative, cumulative + pre_act * density)


def leave_kernel(kept, moved, out):
    out[...] = (kept[1].astype(F32) + moved[1].astype(F32)).astype(BF16)


def adam_kernel(axis, place, kept, moved, there, first, second, step_dir, new_first, new_second):
    size = there.shape[axis]
    here = kept[0].astype(F32) + moved[0].astype(F32)
    for grad, which in ((here, place[2]), (there[...].astype(F32), 1 - place[2])):
        half = pl.ds(pl.multiple_of(which * size, size), size)
        at = (half, slice(None)) if axis == 0 else (slice(None), half)
        first_new = 0.9 * first[at] + 0.1 * grad
        second_new = 0.99 * second[at] + 0.01 * grad * grad
        new_first[at] = first_new
        new_second[at] = second_new
        scaled = jnp.sqrt(second_new * (1.0 / SECOND_FIX)) + 1e-08
        step_dir[at] = (first_new * (1.0 / FIRST_FIX) / scaled).astype(BF16)


def adam_step(axis, place, kept, moved, there, first, second, follows=()):
    return call_kernel(
        functools.partial(adam_kernel, axis),
        [like(first, dtype=BF16), like(first), like(first)],
        [kept, moved, there, first, second],
        scalars=place,
        follows=follows,
    )


def reduce_over_z(parts, long_way, follows=()):
    far = parts[4]
    sums = []
    order = (5, 6, 7) if long_way < 0 else (3, 2, 1)
    for i, k in enumerate(order):
        far = add_rounded(shift_z(far, long_way), parts[k], follows[i : i + 1])
        sums.append(far)
    far = shift_z(far, long_way)
    order = (3, 2, 1) if long_way < 0 else (5, 6, 7)
    near = parts[order[0]]
    for k in order[1:]:
        near = add_rounded(shift_z(near, -long_way), parts[k])
    near = shift_z(near, -long_way)
    return (parts[0], far, near), sums


def gather_over_z(chunk, long_way):
    found = [chunk] + [None] * (NZ - 1)
    far = near = chunk
    for step in range(1, 5):
        far = shift_z(far, long_way)
        found[(-long_way * step) % NZ] = far
        if step < 4:
            near = shift_z(near, -long_way)
            found[(long_way * step) % NZ] = near
    return found


def body(normed, out_grad, w_in, w_out, first_in, second_in, first_out, second_out):
    mx = lax.axis_index("mx")
    y = lax.axis_index("my")
    z, x_hi = mx // 2, mx % 2
    place = jnp.stack([z, y, x_hi]).astype(jnp.int32)
    rows = normed.shape[0] // NY
    width, hid = w_in.shape[0], w_in.shape[1] // 2

    quarter, pair, keep, send, sent = copy_kernel(
        split_kernel,
        [like(normed, (rows, width)), like(normed, (2, rows, width))]
        + [like(w_in, (2, width, hid))] * 2
        + [like(out_grad)],
        place,
        [normed, out_grad, w_in, w_out],
        8,
    )
    quarters = [swap_x_lo(quarter), swap_x_both(quarter), swap_x_hi(pair)]
    send, sent = call_kernel(pass_kernel, [like(send), like(sent)], [send, sent], follows=quarters)
    part = swap_x_hi(send)
    other = swap_core(keep)
    mine = call_kernel(
        stack_kernel, [like(normed, (4, rows, width))], quarters, follows=[other]
    )[0]
    above, below = shift_y(mine, -1), shift_y(mine, 1)
    beside = [swap_x_lo(sent), swap_x_both(sent)]
    up, down = call_kernel(
        forward_kernel, [like(normed, (2, rows, width))] * 2, [below, above], follows=[part]
    )
    tokens = [mine, above, shift_y(up, 1), shift_y(down, -1), below]
    weights = [keep, other, part, swap_core(part)]
    pre_parts, whole_in, weight_in = partial_sums(
        True, place, normed, tokens, weights, beside
    )
    back_parts, whole_out, _ = partial_sums(
        False, place, out_grad, tokens + beside, weights, [pre_parts[4]]
    )
    back_terms, back_sums = reduce_over_z(back_parts, 1)
    pre_terms, _ = reduce_over_z(pre_parts, -1, [back_parts[4], *back_sums[:2]])
    chunk = pre_parts[0]
    act, slope = call_kernel(act_kernel, [like(chunk), like(chunk, dtype=F32)], pre_terms, follows=back_sums[2:])
    acts = gather_over_z(act, 1)
    act_grad = call_kernel(act_grad_kernel, [like(chunk)], [*back_terms, slope])[0]
    act_grads = gather_over_z(act_grad, -1)

    images = float(normed.shape[0] * lax.axis_size("dp") // PATCHES)
    first_places, last_places = (0, 1, 7), (2, 6, 3, 5, 4)
    early = token_grad(place, [act_grads[k] for k in first_places], weight_in)
    terms = send_over_y(early)
    kept_out, swapped = weight_grad(False, 1.0 / images, acts, whole_out, terms[1:])
    moved_out = swap_core(swapped)
    leaving_out = call_kernel(leave_kernel, [like(swapped, (hid, width))], [kept_out, moved_out])[0]
    there_out = swap_x_hi(leaving_out)
    kept_in, swapped = weight_grad(True, 1.0 / images, act_grads, whole_in)
    moved_in = swap_core(swapped)
    late = token_grad(
        place, [act_grads[k] for k in last_places], weight_in, [leaving_out, kept_in]
    )
    terms += send_over_y(late)
    leaving_in = call_kernel(
        leave_kernel, [like(swapped, (width, hid))], [kept_in, moved_in], follows=late[:1]
    )[0]
    there_in = swap_x_hi(leaving_in)
    block = (rows, width)
    own, side, other_side, both = call_kernel(
        sum_kernel, [like(normed, block, F32)] + [like(normed, block)] * 3, terms
    )
    update_out, new_first_out, new_second_out = adam_step(
        0, place, kept_out, moved_out, there_out, first_out, second_out, [own]
    )
    update_in, new_first_in, new_second_in = adam_step(
        1, place, kept_in, moved_in, there_in, first_in, second_in, [update_out]
    )
    input_grad = call_kernel(
        functools.partial(place_kernel, first_places + last_places),
        [like(normed, block)],
        [own, swap_x_lo(other_side), swap_x_hi(side), swap_x_both(both)],
        scalars=place,
    )[0]
    return (
        input_grad,
        update_in,
        new_first_in,
        new_second_in,
        update_out,
        new_first_out,
        new_second_out,
    )


def solution(mesh):
    in_specs = (
        P("dp", "mx"),
        P("dp", "mx"),
        P("mx", ("my", "dp")),
        P(("my", "dp"), "mx"),
        P("mx", ("my", "dp")),
        P("mx", ("my", "dp")),
        P(("my", "dp"), "mx"),
        P(("my", "dp"), "mx"),
    )
    out_specs = (
        P(("dp", "my"), "mx"),
        P("mx", ("my", "dp")),
        P("mx", ("my", "dp")),
        P("mx", ("my", "dp")),
        P(("my", "dp"), "mx"),
        P(("my", "dp"), "mx"),
        P(("my", "dp"), "mx"),
    )
    return jax.shard_map(body, mesh=mesh, in_specs=in_specs, out_specs=out_specs, check_vma=False)
```

```python
import functools

import jax
import jax.numpy as jnp
from jax import lax
from jax.experimental import pallas as pl
from jax.experimental.pallas import tpu as pltpu
from jax.sharding import PartitionSpec as P

PATCHES = 256
NZ = 8
NY = 4
INV_ROOT2 = 0.7071067811865476
INV_ROOT2PI = 0.3989422804014327
FIRST_FIX = 1.0 - 0.9**10
SECOND_FIX = 1.0 - 0.99**10
BF16 = jnp.bfloat16
F32 = jnp.float32
VMEM_BYTES = 24 * 1024 * 1024
WHOLE_VMEM_BYTES = 63 * 1024 * 1024


def swap_core(value):
    return lax.ppermute(value, "dp", [(i, i ^ 1) for i in range(4)])


def swap_x_lo(value):
    return lax.ppermute(value, "dp", [(i, i ^ 2) for i in range(4)])


def swap_x_hi(value):
    return lax.ppermute(value, "mx", [(i, i ^ 1) for i in range(16)])


def swap_x_both(value):
    pairs = [(d * 16 + m, (d ^ 2) * 16 + (m ^ 1)) for d in range(4) for m in range(16)]
    return lax.ppermute(value, ("dp", "mx"), pairs)


def shift_z(value, by):
    return lax.ppermute(value, "mx", [(i, (i + 2 * by) % 16) for i in range(16)])


def shift_y(value, by):
    return lax.ppermute(value, "my", [(i, (i + by) % NY) for i in range(NY)])


def vmem_specs(count):
    return [pl.BlockSpec(memory_space=pltpu.VMEM)] * count


def call_kernel(kernel, out_shapes, operands, scratch=(), flops=0, scalars=None, follows=()):
    operands, follows = list(operands), list(follows)
    moved = sum(o.size * o.dtype.itemsize for o in operands)
    moved += sum(o.size * o.dtype.itemsize for o in out_shapes)
    in_specs = vmem_specs(len(operands))
    in_specs += [pl.BlockSpec(memory_space=pl.ANY)] * len(follows)
    skip, count = len(operands), len(follows)
    operands += follows
    if scalars is not None:
        in_specs = [pl.BlockSpec(memory_space=pltpu.SMEM)] + in_specs
        operands = [scalars] + operands
        skip += 1

    def run(*refs):
        kernel(*refs[:skip], *refs[skip + count :])

    return pl.pallas_call(
        run,
        out_shape=out_shapes,
        in_specs=in_specs,
        out_specs=vmem_specs(len(out_shapes)),
        scratch_shapes=list(scratch),
        compiler_params=pltpu.CompilerParams(vmem_limit_bytes=VMEM_BYTES),
        cost_estimate=pl.CostEstimate(flops=0, bytes_accessed=0, transcendentals=0),
    )(*operands)


def like(array, shape=None, dtype=None):
    return jax.ShapeDtypeStruct(shape or array.shape, dtype or array.dtype)


def copy_all(pairs, sems):
    copies = [pltpu.make_async_copy(src, dst, sems.at[i]) for i, (src, dst) in enumerate(pairs)]
    for copy in copies:
        copy.start()
    for copy in copies:
        copy.wait()


def copy_kernel(kernel, out_shapes, place, operands, copies, follows=(), vmem=VMEM_BYTES):
    count = len(operands)

    def run(place_ref, *refs):
        kernel(place_ref, *refs[:count], *refs[count + len(follows) :])

    return pl.pallas_call(
        run,
        out_shape=out_shapes,
        in_specs=[pl.BlockSpec(memory_space=pltpu.SMEM)]
        + [pl.BlockSpec(memory_space=pltpu.HBM)] * count
        + [pl.BlockSpec(memory_space=pl.ANY)] * len(follows),
        out_specs=vmem_specs(len(out_shapes)),
        scratch_shapes=[pltpu.SemaphoreType.DMA((copies,))],
        compiler_params=pltpu.CompilerParams(vmem_limit_bytes=vmem),
        cost_estimate=pl.CostEstimate(flops=0, bytes_accessed=0, transcendentals=0),
    )(place, *operands, *follows)


def halves_of(weight, axis, size, x_hi):
    views = []
    for which in (x_hi, 1 - x_hi):
        half = pl.ds(pl.multiple_of(which * size, size), size)
        views.append(weight.at[half, :] if axis == 0 else weight.at[:, half])
    return views


def split_kernel(place, tokens, cotangent, w_in, alone, joined, keep_in, sems):
    rows = alone.shape[0]
    line = pl.ds(pl.multiple_of(place[1] * rows, rows), rows)
    mine = tokens.at[line, :]
    stays, goes = halves_of(w_in, 1, keep_in.shape[1], place[2])
    copy_all(
        [
            (mine, alone),
            (mine, joined.at[:rows]),
            (cotangent.at[line, :], joined.at[rows : 2 * rows]),
            (goes, joined.at[2 * rows :]),
            (stays, keep_in),
        ],
        sems,
    )


def half_kernel(place, weight, keep, send, sems):
    stays, goes = halves_of(weight, 0, keep.shape[0], place[2])
    copy_all([(stays, keep), (goes, send)], sems)


def whole_kernel(place, tokens, copied, sems):
    copy_all([(tokens, copied)], sems)


def forward_kernel(before, beyond, up, down):
    size = up.shape[0]
    up[...] = before[:size]
    down[...] = beyond[size:]


def pack_kernel(one, two, out):
    out[0] = one[...]
    out[1] = two[...]


def stack_kernel(one, two, joined, keep, out, pair):
    rows = one.shape[0]
    out[0] = one[...]
    out[1] = two[...]
    out[2] = joined[:rows]
    out[3] = joined[rows : 2 * rows]
    pair[0] = keep[...]
    pair[1] = joined[2 * rows :]


def add_kernel(moving, mine, out):
    out[...] = (moving[...].astype(F32) + mine[...].astype(F32)).astype(BF16)


def add_rounded(moving, mine, follows=()):
    return call_kernel(add_kernel, [like(mine)], [moving, mine], follows=follows)[0]


def act_kernel(own, far, near, act, slope):
    pre_act = own[...].astype(F32) + far[...].astype(F32) + near[...].astype(F32)
    value, slope[...] = gelu_pair(pre_act)
    act[...] = value.astype(BF16)


def act_grad_kernel(own, far, near, slope, out):
    act_back = own[...].astype(F32) + far[...].astype(F32) + near[...].astype(F32)
    out[...] = (act_back * slope[...]).astype(BF16)


def assemble_tokens(place, own, moved, whole, rows, width):
    z, y = place[0], place[1]
    step = rows // NZ

    def put(c, side, yy, right, block):
        k = lax.rem(c + NZ - z, NZ)
        at = pl.multiple_of(((k * 2 + side) * NY + yy) * step, step)
        columns = slice(width, 2 * width) if right else slice(0, width)
        whole[pl.ds(at, step), columns] = block

    beside = moved[NY + 1 :]

    def piece(j, p, line):
        if j == 2:
            half = moved[2].shape[0]
            return moved[2][p, line, :] if p < half else moved[3][p - half, line, :]
        return moved[j + 1 if j > 2 else j][p, line, :]

    for c in range(NZ):
        for yy in range(NY):
            line = slice(yy * rows + c * step, yy * rows + (c + 1) * step)
            put(c, 0, yy, False, own[line, :])
            if beside:
                put(c, 1, yy, False, beside[0][line, :])
                put(c, 1, yy, True, beside[1][line, :])
        line = slice(c * step, (c + 1) * step)
        for j in range(NY):
            yy = lax.rem(y + j, NY)
            if beside:
                put(c, 0, yy, True, piece(j, 3, line))
            else:
                put(c, 1, yy, False, piece(j, 0, line))
                put(c, 1, yy, True, piece(j, 1, line))
                put(c, 0, yy, True, piece(j, 2, line))


def partial_kernel(by_rows, place, own, *refs):
    moved, (near, other) = refs[: -NZ - 4], refs[-NZ - 4 : -NZ - 2]
    out, (whole, weight) = refs[-NZ - 2 : -2], refs[-2:]
    rows, width = own.shape[0] // NY, own.shape[1]
    hid = near.shape[2] if by_rows else near.shape[1]
    assemble_tokens(place, own, moved, whole, rows, width)
    for d in range(2):
        columns = slice(d * width, (d + 1) * width)
        for f, source in enumerate((near, other)):
            units = slice(f * hid, (f + 1) * hid)
            weight[(columns, units) if by_rows else (units, columns)] = source[d]
    contract = (((1,), (0,)), ((), ())) if by_rows else (((1,), (1,)), ((), ()))
    for k in range(0, NZ, 2):
        rows_k = slice(k * rows, (k + 2) * rows)
        both = lax.dot_general(whole[rows_k, :], weight[...], contract, preferred_element_type=F32)
        out[k][...] = both[:rows].astype(BF16)
        out[k + 1][...] = both[rows:].astype(BF16)


def partial_sums(by_rows, place, own, moved, weights, follows=()):
    rows, width = own.shape[0] // NY, own.shape[1]
    hid = weights[0].shape[2 if by_rows else 1]
    outs = [jax.ShapeDtypeStruct((rows, 2 * hid), BF16)] * NZ + [
        jax.ShapeDtypeStruct((NZ * rows, 2 * width), BF16),
        jax.ShapeDtypeStruct((2 * width, 2 * hid) if by_rows else (2 * hid, 2 * width), BF16),
    ]
    flops = 2 * NZ * rows * 2 * width * 2 * hid

    def kernel(*refs):
        partial_kernel(by_rows, *refs)

    results = call_kernel(kernel, outs, [own, *moved, *weights], [], flops, place, follows)
    return results[:NZ], results[NZ], results[NZ + 1]


def grad_kernel(scale, tokens_left, *refs):
    chunks, tokens, outs, whole = refs[:NZ], refs[NZ], refs[NZ + 1 : NZ + 3], refs[NZ + 3]
    rows = chunks[0].shape[0]
    for k in range(NZ):
        whole[k * rows : (k + 1) * rows, :] = chunks[k][...]
    width, hid = outs[0].shape[1:] if tokens_left else outs[0].shape[:0:-1]
    over = (((0,), (0,)), ((), ()))
    for d in range(2):
        for f in range(2):
            units = whole[:, f * hid : (f + 1) * hid]
            columns = tokens[:, d * width : (d + 1) * width]
            left, right = (columns, units) if tokens_left else (units, columns)
            total = lax.dot_general(left, right, over, preferred_element_type=F32)
            outs[f][d] = (total * scale).astype(BF16)


def weight_grad(tokens_left, scale, chunks, tokens, follows=()):
    rows, hid2 = chunks[0].shape
    width2 = tokens.shape[1]
    hid, width = hid2 // 2, width2 // 2
    tail = (width, hid) if tokens_left else (hid, width)
    outs = [jax.ShapeDtypeStruct((2,) + tail, BF16)] * 2
    flops = 2 * NZ * rows * hid2 * width2

    def kernel(*refs):
        grad_kernel(scale, tokens_left, *refs)

    scratch = [pltpu.VMEM((NZ * rows, hid2), BF16)]
    return call_kernel(kernel, outs, [*chunks, tokens], scratch, flops, follows=follows)


def back_kernel(count, place, *refs):
    chunks, weight = refs[:count], refs[count]
    outs, whole, total = refs[count + 1 : count + 1 + NY], refs[-2], refs[-1]
    y = place[1]
    rows = chunks[0].shape[0]
    step = rows // NZ
    width = outs[0].shape[3]
    for k in range(count):
        whole[k * rows : (k + 1) * rows, :] = chunks[k][...]
    total[...] = lax.dot_general(
        whole[...], weight[...], (((1,), (1,)), ((), ())), preferred_element_type=F32
    ).astype(BF16)
    for j in range(NY):
        yy = lax.rem(y + j, NY)
        for k in range(count):
            for side in range(2):
                at = pl.multiple_of(((k * 2 + side) * NY + yy) * step, step)
                line = slice(k * step, (k + 1) * step)
                for d in range(2):
                    columns = slice(d * width, (d + 1) * width)
                    outs[j][side, d, line, :] = total[pl.ds(at, step), columns]


def token_grad(place, chunks, weight, follows=()):
    count = len(chunks)
    rows, hid2 = chunks[0].shape
    width2 = weight.shape[0]
    outs = [jax.ShapeDtypeStruct((2, 2, count * rows // NZ, width2 // 2), BF16)] * NY
    flops = 2 * count * rows * hid2 * width2
    scratch = [pltpu.VMEM((count * rows, hid2), BF16), pltpu.VMEM((count * rows, width2), BF16)]

    def kernel(*refs):
        back_kernel(count, *refs)

    return call_kernel(kernel, outs, [*chunks, weight], scratch, flops, place, follows)


def send_over_y(outs):
    return [outs[0], shift_y(outs[1], 1), shift_y(outs[2], 2), shift_y(outs[3], 3)]


def sum_kernel(*refs):
    terms, outs = refs[:-4], refs[-4:]
    at = 0
    for group in (terms[:NY], terms[NY:]):
        size = group[0].shape[2]
        for side in range(2):
            for d in range(2):
                total = sum(term[side, d].astype(F32) for term in group)
                out = outs[side * 2 + d]
                out[at : at + size, :] = total.astype(out.dtype)
        at += size


def place_kernel(order, place, own, one, two, three, out):
    z = place[0]
    step = out.shape[0] // NZ
    for i, k in enumerate(order):
        line = slice(i * step, (i + 1) * step)
        total = own[line, :] + one[line, :].astype(F32)
        total += two[line, :].astype(F32) + three[line, :].astype(F32)
        at = pl.multiple_of(lax.rem(z + k, NZ) * step, step)
        out[pl.ds(at, step), :] = total.astype(BF16)


def gelu_pair(pre_act):
    cumulative = 0.5 * (1.0 + jax.scipy.special.erf(pre_act * INV_ROOT2))
    density = jnp.exp(-0.5 * pre_act * pre_act) * INV_ROOT2PI
    return (pre_act * cumulative, cumulative + pre_act * density)


def leave_kernel(kept, moved, out):
    out[...] = (kept[1].astype(F32) + moved[1].astype(F32)).astype(BF16)


def adam_kernel(place, kept, moved, there, first, second, step_dir, new_first, new_second):
    def update(grad):
        first_new = 0.9 * first[...] + 0.1 * grad
        second_new = 0.99 * second[...] + 0.01 * grad * grad
        new_first[...] = first_new
        new_second[...] = second_new
        scaled = jnp.sqrt(second_new * (1.0 / SECOND_FIX)) + 1e-08
        step_dir[...] = (first_new * (1.0 / FIRST_FIX) / scaled).astype(BF16)

    @pl.when(pl.program_id(0) == 0)
    def _():
        update(kept[0].astype(F32) + moved[0].astype(F32))

    @pl.when(pl.program_id(0) == 1)
    def _():
        update(there[...].astype(F32))


ADAM_STEPS = 4


def adam_step(axis, place, kept, moved, there, first, second, follows=()):
    rows, columns = there.shape
    block = (rows // ADAM_STEPS, columns)

    def at(half, step, p):
        which = jnp.where(half == 0, p[2], 1 - p[2])
        return (which * ADAM_STEPS + step, 0) if axis == 0 else (step, which)

    def run(place_ref, *refs):
        adam_kernel(place_ref, *refs[:5], *refs[5 + len(follows) :])

    pair = pl.BlockSpec((2,) + block, lambda i, j, p: (0, jnp.where(i == 0, j, ADAM_STEPS - 1), 0))
    alone = pl.BlockSpec(block, lambda i, j, p: (jnp.where(i == 0, 0, j), 0))
    moment = pl.BlockSpec(block, at)
    outs = [like(first, dtype=BF16), like(first), like(first)]
    return pl.pallas_call(
        run,
        out_shape=outs,
        grid_spec=pltpu.PrefetchScalarGridSpec(
            num_scalar_prefetch=1,
            grid=(2, ADAM_STEPS),
            in_specs=[pair, pair, alone, moment, moment]
            + [pl.BlockSpec(memory_space=pl.ANY)] * len(follows),
            out_specs=[moment] * 3,
        ),
        compiler_params=pltpu.CompilerParams(vmem_limit_bytes=VMEM_BYTES),
        cost_estimate=pl.CostEstimate(flops=0, bytes_accessed=0, transcendentals=0),
    )(place, kept, moved, there, first, second, *follows)


def reduce_over_z(parts, long_way, follows=()):
    far = parts[4]
    sums = []
    order = (5, 6, 7) if long_way < 0 else (3, 2, 1)
    for i, k in enumerate(order):
        far = add_rounded(shift_z(far, long_way), parts[k], [f for f in follows[i : i + 1] if f is not None])
        sums.append(far)
    far = shift_z(far, long_way)
    order = (3, 2, 1) if long_way < 0 else (5, 6, 7)
    near = parts[order[0]]
    for k in order[1:]:
        near = add_rounded(shift_z(near, -long_way), parts[k])
    near = shift_z(near, -long_way)
    return (parts[0], far, near), sums


def gather_over_z(chunk, long_way):
    found = [chunk] + [None] * (NZ - 1)
    far = near = chunk
    for step in range(1, 5):
        far = shift_z(far, long_way)
        found[(-long_way * step) % NZ] = far
        if step < 4:
            near = shift_z(near, -long_way)
            found[(long_way * step) % NZ] = near
    return found


def body(normed, out_grad, w_in, w_out, first_in, second_in, first_out, second_out):
    mx = lax.axis_index("mx")
    y = lax.axis_index("my")
    z, x_hi = mx // 2, mx % 2
    place = jnp.stack([z, y, x_hi]).astype(jnp.int32)
    rows = normed.shape[0] // NY
    width, hid = w_in.shape[0], w_in.shape[1] // 2

    quarter, joined, keep_in = copy_kernel(
        split_kernel,
        [like(normed, (rows, width)), like(normed, (2 * rows + width, width))]
        + [like(w_in, (width, hid))],
        place,
        [normed, out_grad, w_in],
        5,
        vmem=WHOLE_VMEM_BYTES,
    )
    quarters = [swap_x_lo(quarter), swap_x_both(quarter), swap_x_hi(joined)]
    mine, pair_in = call_kernel(
        stack_kernel,
        [like(normed, (4, rows, width)), like(keep_in, (2, width, hid))],
        [*quarters, keep_in],
    )
    above, below = shift_y(mine, -1), shift_y(mine, 1)
    (sent,) = copy_kernel(whole_kernel, [like(out_grad)], place, [out_grad], 1, [mine])
    beside = [swap_x_lo(sent), swap_x_both(sent)]
    keep_out, send_out = copy_kernel(
        half_kernel, [like(w_out, (hid, width))] * 2, place, [w_out], 2, [above, below, *beside]
    )
    part_out = swap_x_hi(send_out)
    weights_in = [pair_in, swap_core(pair_in)]
    up, down = call_kernel(
        forward_kernel, [like(normed, (2, rows, width))] * 2, [below, above], follows=beside
    )
    tokens = [mine, above, shift_y(up, 1), shift_y(down, -1), below]
    (pair_out,) = call_kernel(
        pack_kernel, [like(keep_out, (2, hid, width))], [keep_out, part_out], follows=tokens[2:4]
    )
    weights_out = [pair_out, swap_core(pair_out)]
    pre_parts, whole_in, weight_in = partial_sums(True, place, normed, tokens, weights_in)
    back_parts, whole_out, _ = partial_sums(
        False, place, out_grad, tokens + beside, weights_out, [pre_parts[4]]
    )
    back_terms, back_sums = reduce_over_z(back_parts, 1)
    pre_terms, _ = reduce_over_z(pre_parts, -1, [None, back_parts[4], back_sums[0]])
    chunk = pre_parts[0]
    act, slope = call_kernel(act_kernel, [like(chunk), like(chunk, dtype=F32)], pre_terms, follows=back_sums[1:2])
    acts = gather_over_z(act, 1)
    act_grad = call_kernel(act_grad_kernel, [like(chunk)], [*back_terms, slope])[0]
    act_grads = gather_over_z(act_grad, -1)

    images = float(normed.shape[0] * lax.axis_size("dp") // PATCHES)
    first_places, last_places = (0, 1, 7), (2, 6, 3, 5, 4)
    early = token_grad(place, [act_grads[k] for k in first_places], weight_in)
    terms = send_over_y(early)
    kept_out, swapped = weight_grad(False, 1.0 / images, acts, whole_out, terms[1:])
    moved_out = swap_core(swapped)
    leaving_out = call_kernel(leave_kernel, [like(swapped, (hid, width))], [kept_out, moved_out])[0]
    there_out = swap_x_hi(leaving_out)
    kept_in, swapped = weight_grad(True, 1.0 / images, act_grads, whole_in)
    moved_in = swap_core(swapped)
    late = token_grad(
        place, [act_grads[k] for k in last_places], weight_in, [leaving_out, kept_in]
    )
    terms += send_over_y(late)
    leaving_in = call_kernel(
        leave_kernel, [like(swapped, (width, hid))], [kept_in, moved_in], follows=late[:1]
    )[0]
    there_in = swap_x_hi(leaving_in)
    update_out, new_first_out, new_second_out = adam_step(
        0, place, kept_out, moved_out, there_out, first_out, second_out, [leaving_in]
    )
    block = (rows, width)
    own, side, other_side, both = call_kernel(
        sum_kernel, [like(normed, block, F32)] + [like(normed, block)] * 3, terms, follows=[update_out]
    )
    update_in, new_first_in, new_second_in = adam_step(
        1, place, kept_in, moved_in, there_in, first_in, second_in, [own]
    )
    input_grad = call_kernel(
        functools.partial(place_kernel, first_places + last_places),
        [like(normed, block)],
        [own, swap_x_lo(other_side), swap_x_hi(side), swap_x_both(both)],
        scalars=place,
    )[0]
    return (
        input_grad,
        update_in,
        new_first_in,
        new_second_in,
        update_out,
        new_first_out,
        new_second_out,
    )


def solution(mesh):
    in_specs = (
        P("dp", "mx"),
        P("dp", "mx"),
        P("mx", ("my", "dp")),
        P(("my", "dp"), "mx"),
        P("mx", ("my", "dp")),
        P("mx", ("my", "dp")),
        P(("my", "dp"), "mx"),
        P(("my", "dp"), "mx"),
    )
    out_specs = (
        P(("dp", "my"), "mx"),
        P("mx", ("my", "dp")),
        P("mx", ("my", "dp")),
        P("mx", ("my", "dp")),
        P(("my", "dp"), "mx"),
        P(("my", "dp"), "mx"),
        P(("my", "dp"), "mx"),
    )
    return jax.shard_map(body, mesh=mesh, in_specs=in_specs, out_specs=out_specs, check_vma=False)
```

```python
import functools

import jax
import jax.numpy as jnp
from jax import lax
from jax.experimental import pallas as pl
from jax.experimental.pallas import tpu as pltpu
from jax.sharding import PartitionSpec as P

PATCHES = 256
NZ = 8
NY = 4
INV_ROOT2 = 0.7071067811865476
INV_ROOT2PI = 0.3989422804014327
FIRST_FIX = 1.0 - 0.9**10
SECOND_FIX = 1.0 - 0.99**10
BF16 = jnp.bfloat16
F32 = jnp.float32
VMEM_BYTES = 24 * 1024 * 1024
WHOLE_VMEM_BYTES = 63 * 1024 * 1024


def swap_core(value):
    return lax.ppermute(value, "dp", [(i, i ^ 1) for i in range(4)])


def swap_x_lo(value):
    return lax.ppermute(value, "dp", [(i, i ^ 2) for i in range(4)])


def swap_x_hi(value):
    return lax.ppermute(value, "mx", [(i, i ^ 1) for i in range(16)])


def swap_x_both(value):
    pairs = [(d * 16 + m, (d ^ 2) * 16 + (m ^ 1)) for d in range(4) for m in range(16)]
    return lax.ppermute(value, ("dp", "mx"), pairs)


def shift_z(value, by):
    return lax.ppermute(value, "mx", [(i, (i + 2 * by) % 16) for i in range(16)])


def shift_y(value, by):
    return lax.ppermute(value, "my", [(i, (i + by) % NY) for i in range(NY)])


def vmem_specs(count):
    return [pl.BlockSpec(memory_space=pltpu.VMEM)] * count


def call_kernel(kernel, out_shapes, operands, scratch=(), flops=0, scalars=None, follows=()):
    operands, follows = list(operands), list(follows)
    moved = sum(o.size * o.dtype.itemsize for o in operands)
    moved += sum(o.size * o.dtype.itemsize for o in out_shapes)
    in_specs = vmem_specs(len(operands))
    in_specs += [pl.BlockSpec(memory_space=pl.ANY)] * len(follows)
    skip, count = len(operands), len(follows)
    operands += follows
    if scalars is not None:
        in_specs = [pl.BlockSpec(memory_space=pltpu.SMEM)] + in_specs
        operands = [scalars] + operands
        skip += 1

    def run(*refs):
        kernel(*refs[:skip], *refs[skip + count :])

    return pl.pallas_call(
        run,
        out_shape=out_shapes,
        in_specs=in_specs,
        out_specs=vmem_specs(len(out_shapes)),
        scratch_shapes=list(scratch),
        compiler_params=pltpu.CompilerParams(vmem_limit_bytes=VMEM_BYTES),
        cost_estimate=pl.CostEstimate(flops=0, bytes_accessed=0, transcendentals=0),
    )(*operands)


def like(array, shape=None, dtype=None):
    return jax.ShapeDtypeStruct(shape or array.shape, dtype or array.dtype)


def copy_all(pairs, sems):
    copies = [pltpu.make_async_copy(src, dst, sems.at[i]) for i, (src, dst) in enumerate(pairs)]
    for copy in copies:
        copy.start()
    for copy in copies:
        copy.wait()


def copy_kernel(kernel, out_shapes, place, operands, copies, follows=(), vmem=VMEM_BYTES):
    count = len(operands)

    def run(place_ref, *refs):
        kernel(place_ref, *refs[:count], *refs[count + len(follows) :])

    return pl.pallas_call(
        run,
        out_shape=out_shapes,
        in_specs=[pl.BlockSpec(memory_space=pltpu.SMEM)]
        + [pl.BlockSpec(memory_space=pltpu.HBM)] * count
        + [pl.BlockSpec(memory_space=pl.ANY)] * len(follows),
        out_specs=vmem_specs(len(out_shapes)),
        scratch_shapes=[pltpu.SemaphoreType.DMA((copies,))],
        compiler_params=pltpu.CompilerParams(vmem_limit_bytes=vmem),
        cost_estimate=pl.CostEstimate(flops=0, bytes_accessed=0, transcendentals=0),
    )(place, *operands, *follows)


def halves_of(weight, axis, size, x_hi):
    views = []
    for which in (x_hi, 1 - x_hi):
        half = pl.ds(pl.multiple_of(which * size, size), size)
        views.append(weight.at[half, :] if axis == 0 else weight.at[:, half])
    return views


def quarter_kernel(place, tokens, cotangent, pair, sems):
    rows = pair.shape[1]
    line = pl.ds(pl.multiple_of(place[1] * rows, rows), rows)
    copy_all([(tokens.at[line, :], pair.at[0]), (cotangent.at[line, :], pair.at[1])], sems)


def half_kernel(place, w_in, w_out, keep, send, sems):
    size = keep.shape[1]
    stays_in, goes_in = halves_of(w_in, 1, size, place[2])
    stays_out, goes_out = halves_of(w_out, 0, size, place[2])
    copy_all(
        [
            (goes_in, send.at[0]),
            (goes_out, send.at[1]),
            (stays_in, keep.at[0]),
            (stays_out, keep.at[1]),
        ],
        sems,
    )


def forward_kernel(before, beyond, up, down):
    size = up.shape[0]
    up[...] = before[:size]
    down[...] = beyond[size:]


def stack_kernel(one, two, three, send, out, passed):
    for array in range(2):
        for p, source in enumerate((one, two, three)):
            out[3 * array + p] = source[array]
    passed[...] = send[...]


def add_kernel(moving, mine, out):
    out[...] = (moving[...].astype(F32) + mine[...].astype(F32)).astype(BF16)


def add_rounded(moving, mine, follows=()):
    return call_kernel(add_kernel, [like(mine)], [moving, mine], follows=follows)[0]


def act_kernel(own, far, near, act, slope):
    pre_act = own[...].astype(F32) + far[...].astype(F32) + near[...].astype(F32)
    value, slope[...] = gelu_pair(pre_act)
    act[...] = value.astype(BF16)


def act_grad_kernel(own, far, near, slope, out):
    act_back = own[...].astype(F32) + far[...].astype(F32) + near[...].astype(F32)
    out[...] = (act_back * slope[...]).astype(BF16)


def assemble_tokens(place, own, moved, first, whole, rows, width):
    z, y = place[0], place[1]
    step = rows // NZ

    def put(c, side, yy, right, block):
        k = lax.rem(c + NZ - z, NZ)
        at = pl.multiple_of(((k * 2 + side) * NY + yy) * step, step)
        columns = slice(width, 2 * width) if right else slice(0, width)
        whole[pl.ds(at, step), columns] = block

    for c in range(NZ):
        for yy in range(NY):
            put(c, 0, yy, False, own[yy * rows + c * step : yy * rows + (c + 1) * step, :])
        line = slice(c * step, (c + 1) * step)
        for j in range(NY):
            yy = lax.rem(y + j, NY)
            skip = 0 if moved[j].shape[0] == 3 else first
            put(c, 1, yy, False, moved[j][skip, line, :])
            put(c, 1, yy, True, moved[j][skip + 1, line, :])
            put(c, 0, yy, True, moved[j][skip + 2, line, :])


def partial_kernel(by_rows, place, own, *refs):
    moved, sources = refs[:NY], refs[NY : NY + 4]
    out, (whole, weight) = refs[NY + 4 : -2], refs[-2:]
    which = 0 if by_rows else 1
    rows, width = own.shape[0] // NY, own.shape[1]
    hid = sources[0].shape[2] if by_rows else sources[0].shape[1]
    assemble_tokens(place, own, moved, 3 * which, whole, rows, width)
    for d in range(2):
        columns = slice(d * width, (d + 1) * width)
        for f in range(2):
            units = slice(f * hid, (f + 1) * hid)
            weight[(columns, units) if by_rows else (units, columns)] = sources[2 * d + f][which]
    contract = (((1,), (0,)), ((), ())) if by_rows else (((1,), (1,)), ((), ()))
    for k in range(0, NZ, 2):
        rows_k = slice(k * rows, (k + 2) * rows)
        both = lax.dot_general(whole[rows_k, :], weight[...], contract, preferred_element_type=F32)
        out[k][...] = both[:rows].astype(BF16)
        out[k + 1][...] = both[rows:].astype(BF16)


def partial_sums(by_rows, place, own, moved, weights, follows=()):
    rows, width = own.shape[0] // NY, own.shape[1]
    hid = weights[0].shape[2 if by_rows else 1]
    outs = [jax.ShapeDtypeStruct((rows, 2 * hid), BF16)] * NZ + [
        jax.ShapeDtypeStruct((NZ * rows, 2 * width), BF16),
        jax.ShapeDtypeStruct((2 * width, 2 * hid) if by_rows else (2 * hid, 2 * width), BF16),
    ]
    flops = 2 * NZ * rows * 2 * width * 2 * hid

    def kernel(*refs):
        partial_kernel(by_rows, *refs)

    results = call_kernel(kernel, outs, [own, *moved, *weights], [], flops, place, follows)
    return results[:NZ], results[NZ], results[NZ + 1]


def grad_kernel(scale, tokens_left, *refs):
    chunks, tokens, outs, whole = refs[:NZ], refs[NZ], refs[NZ + 1 : NZ + 3], refs[NZ + 3]
    rows = chunks[0].shape[0]
    for k in range(NZ):
        whole[k * rows : (k + 1) * rows, :] = chunks[k][...]
    width, hid = outs[0].shape[1:] if tokens_left else outs[0].shape[:0:-1]
    over = (((0,), (0,)), ((), ()))
    for d in range(2):
        for f in range(2):
            units = whole[:, f * hid : (f + 1) * hid]
            columns = tokens[:, d * width : (d + 1) * width]
            left, right = (columns, units) if tokens_left else (units, columns)
            total = lax.dot_general(left, right, over, preferred_element_type=F32)
            outs[f][d] = (total * scale).astype(BF16)


def weight_grad(tokens_left, scale, chunks, tokens, follows=()):
    rows, hid2 = chunks[0].shape
    width2 = tokens.shape[1]
    hid, width = hid2 // 2, width2 // 2
    tail = (width, hid) if tokens_left else (hid, width)
    outs = [jax.ShapeDtypeStruct((2,) + tail, BF16)] * 2
    flops = 2 * NZ * rows * hid2 * width2

    def kernel(*refs):
        grad_kernel(scale, tokens_left, *refs)

    scratch = [pltpu.VMEM((NZ * rows, hid2), BF16)]
    return call_kernel(kernel, outs, [*chunks, tokens], scratch, flops, follows=follows)


def back_kernel(count, place, *refs):
    chunks, weight = refs[:count], refs[count]
    outs, whole, total = refs[count + 1 : count + 1 + NY], refs[-2], refs[-1]
    y = place[1]
    rows = chunks[0].shape[0]
    step = rows // NZ
    width = outs[0].shape[3]
    for k in range(count):
        whole[k * rows : (k + 1) * rows, :] = chunks[k][...]
    total[...] = lax.dot_general(
        whole[...], weight[...], (((1,), (1,)), ((), ())), preferred_element_type=F32
    ).astype(BF16)
    for j in range(NY):
        yy = lax.rem(y + j, NY)
        for k in range(count):
            for side in range(2):
                at = pl.multiple_of(((k * 2 + side) * NY + yy) * step, step)
                line = slice(k * step, (k + 1) * step)
                for d in range(2):
                    columns = slice(d * width, (d + 1) * width)
                    outs[j][side, d, line, :] = total[pl.ds(at, step), columns]


def token_grad(place, chunks, weight, follows=()):
    count = len(chunks)
    rows, hid2 = chunks[0].shape
    width2 = weight.shape[0]
    outs = [jax.ShapeDtypeStruct((2, 2, count * rows // NZ, width2 // 2), BF16)] * NY
    flops = 2 * count * rows * hid2 * width2
    scratch = [pltpu.VMEM((count * rows, hid2), BF16), pltpu.VMEM((count * rows, width2), BF16)]

    def kernel(*refs):
        back_kernel(count, *refs)

    return call_kernel(kernel, outs, [*chunks, weight], scratch, flops, place, follows)


def send_over_y(outs):
    return [outs[0], shift_y(outs[1], 1), shift_y(outs[2], 2), shift_y(outs[3], 3)]


def sum_kernel(*refs):
    terms, outs = refs[:-4], refs[-4:]
    at = 0
    for group in (terms[:NY], terms[NY:]):
        size = group[0].shape[2]
        for side in range(2):
            for d in range(2):
                total = sum(term[side, d].astype(F32) for term in group)
                out = outs[side * 2 + d]
                out[at : at + size, :] = total.astype(out.dtype)
        at += size


def place_kernel(order, place, own, one, two, three, out):
    z = place[0]
    step = out.shape[0] // NZ
    for i, k in enumerate(order):
        line = slice(i * step, (i + 1) * step)
        total = own[line, :] + one[line, :].astype(F32)
        total += two[line, :].astype(F32) + three[line, :].astype(F32)
        at = pl.multiple_of(lax.rem(z + k, NZ) * step, step)
        out[pl.ds(at, step), :] = total.astype(BF16)


def gelu_pair(pre_act):
    cumulative = 0.5 * (1.0 + jax.scipy.special.erf(pre_act * INV_ROOT2))
    density = jnp.exp(-0.5 * pre_act * pre_act) * INV_ROOT2PI
    return (pre_act * cumulative, cumulative + pre_act * density)


def leave_kernel(kept, moved, out):
    out[...] = (kept[1].astype(F32) + moved[1].astype(F32)).astype(BF16)


def adam_kernel(axis, place, kept, moved, there, first, second, step_dir, new_first, new_second):
    size = there.shape[axis]
    rows = there.shape[0]
    block = rows // ADAM_STEPS
    for local, which in ((True, place[2]), (False, 1 - place[2])):
        start = pl.multiple_of(which * size, size)
        for step in range(ADAM_STEPS):
            line = slice(step * block, (step + 1) * block)
            if local:
                grad = kept[0, line, :].astype(F32) + moved[0, line, :].astype(F32)
            else:
                grad = there[line, :].astype(F32)
            at = (pl.ds(start + step * block, block), slice(None))
            if axis == 1:
                at = (line, pl.ds(start, size))
            first_new = 0.9 * first[at] + 0.1 * grad
            second_new = 0.99 * second[at] + 0.01 * grad * grad
            new_first[at] = first_new
            new_second[at] = second_new
            scaled = second_new * (1.0 / SECOND_FIX)
            scaled = scaled * lax.rsqrt(scaled) + 1e-08
            step_dir[at] = (first_new * (1.0 / FIRST_FIX) / scaled).astype(BF16)


ADAM_STEPS = 4


def adam_step(axis, place, kept, moved, there, first, second, follows=()):
    return call_kernel(
        functools.partial(adam_kernel, axis),
        [like(first, dtype=BF16), like(first), like(first)],
        [kept, moved, there, first, second],
        scalars=place,
        follows=follows,
    )


def reduce_over_z(parts, long_way, follows=()):
    far = parts[4]
    sums = []
    order = (5, 6, 7) if long_way < 0 else (3, 2, 1)
    for i, k in enumerate(order):
        far = add_rounded(shift_z(far, long_way), parts[k], [f for f in follows[i : i + 1] if f is not None])
        sums.append(far)
    far = shift_z(far, long_way)
    order = (3, 2, 1) if long_way < 0 else (5, 6, 7)
    near = parts[order[0]]
    for k in order[1:]:
        near = add_rounded(shift_z(near, -long_way), parts[k])
    near = shift_z(near, -long_way)
    return (parts[0], far, near), sums


def gather_over_z(chunk, long_way):
    found = [chunk] + [None] * (NZ - 1)
    far = near = chunk
    for step in range(1, 5):
        far = shift_z(far, long_way)
        found[(-long_way * step) % NZ] = far
        if step < 4:
            near = shift_z(near, -long_way)
            found[(long_way * step) % NZ] = near
    return found


def body(normed, out_grad, w_in, w_out, first_in, second_in, first_out, second_out):
    mx = lax.axis_index("mx")
    y = lax.axis_index("my")
    z, x_hi = mx // 2, mx % 2
    place = jnp.stack([z, y, x_hi]).astype(jnp.int32)
    rows = normed.shape[0] // NY
    width, hid = w_in.shape[0], w_in.shape[1] // 2

    (pair,) = copy_kernel(
        quarter_kernel,
        [like(normed, (2, rows, width))],
        place,
        [normed, out_grad],
        2,
        vmem=WHOLE_VMEM_BYTES,
    )
    keep, send = copy_kernel(half_kernel, [like(w_in, (2, width, hid))] * 2, place, [w_in, w_out], 4)
    mine, send = call_kernel(
        stack_kernel,
        [like(normed, (6, rows, width)), like(send)],
        [swap_x_lo(pair), swap_x_both(pair), swap_x_hi(pair), send],
    )
    part = swap_x_hi(send)
    above, below = shift_y(mine, -1), shift_y(mine, 1)
    up, down = call_kernel(
        forward_kernel, [like(normed, (3, rows, width))] * 2, [below, above]
    )
    weights = [keep, swap_core(keep), part, swap_core(part)]
    pre_parts, whole_in, weight_in = partial_sums(
        True, place, normed, [mine, above, shift_y(up, 1), below], weights
    )
    back_parts, whole_out, _ = partial_sums(
        False, place, out_grad, [mine, above, shift_y(down, -1), below], weights, [pre_parts[4]]
    )
    back_terms, back_sums = reduce_over_z(back_parts, 1)
    pre_terms, _ = reduce_over_z(pre_parts, -1, [None, back_parts[4], back_sums[0]])
    chunk = pre_parts[0]
    act, slope = call_kernel(act_kernel, [like(chunk), like(chunk, dtype=F32)], pre_terms, follows=back_sums[1:2])
    acts = gather_over_z(act, 1)
    act_grad = call_kernel(act_grad_kernel, [like(chunk)], [*back_terms, slope])[0]
    act_grads = gather_over_z(act_grad, -1)

    images = float(normed.shape[0] * lax.axis_size("dp") // PATCHES)
    first_places, last_places = (0, 1, 7), (2, 6, 3, 5, 4)
    early = token_grad(place, [act_grads[k] for k in first_places], weight_in)
    terms = send_over_y(early)
    kept_out, swapped = weight_grad(False, 1.0 / images, acts, whole_out, terms[1:])
    moved_out = swap_core(swapped)
    leaving_out = call_kernel(leave_kernel, [like(swapped, (hid, width))], [kept_out, moved_out])[0]
    there_out = swap_x_hi(leaving_out)
    kept_in, swapped = weight_grad(True, 1.0 / images, act_grads, whole_in)
    moved_in = swap_core(swapped)
    late = token_grad(
        place, [act_grads[k] for k in last_places], weight_in, [leaving_out, kept_in]
    )
    terms += send_over_y(late)
    leaving_in = call_kernel(
        leave_kernel, [like(swapped, (width, hid))], [kept_in, moved_in], follows=late[:1]
    )[0]
    there_in = swap_x_hi(leaving_in)
    update_out, new_first_out, new_second_out = adam_step(
        0, place, kept_out, moved_out, there_out, first_out, second_out, [leaving_in]
    )
    block = (rows, width)
    own, side, other_side, both = call_kernel(
        sum_kernel, [like(normed, block, F32)] + [like(normed, block)] * 3, terms, follows=[update_out]
    )
    update_in, new_first_in, new_second_in = adam_step(
        1, place, kept_in, moved_in, there_in, first_in, second_in, [own]
    )
    input_grad = call_kernel(
        functools.partial(place_kernel, first_places + last_places),
        [like(normed, block)],
        [own, swap_x_lo(other_side), swap_x_hi(side), swap_x_both(both)],
        scalars=place,
        follows=[update_in],
    )[0]
    return (
        input_grad,
        update_in,
        new_first_in,
        new_second_in,
        update_out,
        new_first_out,
        new_second_out,
    )


def solution(mesh):
    in_specs = (
        P("dp", "mx"),
        P("dp", "mx"),
        P("mx", ("my", "dp")),
        P(("my", "dp"), "mx"),
        P("mx", ("my", "dp")),
        P("mx", ("my", "dp")),
        P(("my", "dp"), "mx"),
        P(("my", "dp"), "mx"),
    )
    out_specs = (
        P(("dp", "my"), "mx"),
        P("mx", ("my", "dp")),
        P("mx", ("my", "dp")),
        P("mx", ("my", "dp")),
        P(("my", "dp"), "mx"),
        P(("my", "dp"), "mx"),
        P(("my", "dp"), "mx"),
    )
    return jax.shard_map(body, mesh=mesh, in_specs=in_specs, out_specs=out_specs, check_vma=False)
```

```python
import functools

import jax
import jax.numpy as jnp
from jax import lax
from jax.experimental import pallas as pl
from jax.experimental.pallas import tpu as pltpu
from jax.sharding import PartitionSpec as P

PATCHES = 256
NZ = 8
NY = 4
INV_ROOT2 = 0.7071067811865476
INV_ROOT2PI = 0.3989422804014327
FIRST_FIX = 1.0 - 0.9**10
SECOND_FIX = 1.0 - 0.99**10
BF16 = jnp.bfloat16
F32 = jnp.float32
VMEM_BYTES = 24 * 1024 * 1024
WHOLE_VMEM_BYTES = 63 * 1024 * 1024


def swap_core(value):
    return lax.ppermute(value, "dp", [(i, i ^ 1) for i in range(4)])


def swap_x_lo(value):
    return lax.ppermute(value, "dp", [(i, i ^ 2) for i in range(4)])


def swap_x_hi(value):
    return lax.ppermute(value, "mx", [(i, i ^ 1) for i in range(16)])


def swap_x_both(value):
    pairs = [(d * 16 + m, (d ^ 2) * 16 + (m ^ 1)) for d in range(4) for m in range(16)]
    return lax.ppermute(value, ("dp", "mx"), pairs)


def shift_z(value, by):
    return lax.ppermute(value, "mx", [(i, (i + 2 * by) % 16) for i in range(16)])


def shift_y(value, by):
    return lax.ppermute(value, "my", [(i, (i + by) % NY) for i in range(NY)])


def vmem_specs(count):
    return [pl.BlockSpec(memory_space=pltpu.VMEM)] * count


def call_kernel(kernel, out_shapes, operands, scratch=(), scalars=None, follows=()):
    operands, follows = list(operands), list(follows)
    moved = sum(o.size * o.dtype.itemsize for o in operands)
    moved += sum(o.size * o.dtype.itemsize for o in out_shapes)
    in_specs = vmem_specs(len(operands))
    in_specs += [pl.BlockSpec(memory_space=pl.ANY)] * len(follows)
    skip, count = len(operands), len(follows)
    operands += follows
    if scalars is not None:
        in_specs = [pl.BlockSpec(memory_space=pltpu.SMEM)] + in_specs
        operands = [scalars] + operands
        skip += 1

    def run(*refs):
        kernel(*refs[:skip], *refs[skip + count :])

    return pl.pallas_call(
        run,
        out_shape=out_shapes,
        in_specs=in_specs,
        out_specs=vmem_specs(len(out_shapes)),
        scratch_shapes=list(scratch),
        compiler_params=pltpu.CompilerParams(vmem_limit_bytes=VMEM_BYTES),
        cost_estimate=pl.CostEstimate(flops=0, bytes_accessed=0, transcendentals=0),
    )(*operands)


def like(array, shape=None, dtype=None):
    return jax.ShapeDtypeStruct(shape or array.shape, dtype or array.dtype)


def copy_all(pairs, sems):
    copies = [pltpu.make_async_copy(src, dst, sems.at[i]) for i, (src, dst) in enumerate(pairs)]
    for copy in copies:
        copy.start()
    for copy in copies:
        copy.wait()


def copy_kernel(kernel, out_shapes, place, operands, copies, follows=(), vmem=VMEM_BYTES):
    count = len(operands)

    def run(place_ref, *refs):
        kernel(place_ref, *refs[:count], *refs[count + len(follows) :])

    return pl.pallas_call(
        run,
        out_shape=out_shapes,
        in_specs=[pl.BlockSpec(memory_space=pltpu.SMEM)]
        + [pl.BlockSpec(memory_space=pltpu.HBM)] * count
        + [pl.BlockSpec(memory_space=pl.ANY)] * len(follows),
        out_specs=vmem_specs(len(out_shapes)),
        scratch_shapes=[pltpu.SemaphoreType.DMA((copies,))],
        compiler_params=pltpu.CompilerParams(vmem_limit_bytes=vmem),
        cost_estimate=pl.CostEstimate(flops=0, bytes_accessed=0, transcendentals=0),
    )(place, *operands, *follows)


def halves_of(weight, axis, size, x_hi):
    views = []
    for which in (x_hi, 1 - x_hi):
        half = pl.ds(pl.multiple_of(which * size, size), size)
        views.append(weight.at[half, :] if axis == 0 else weight.at[:, half])
    return views


def quarter_kernel(place, tokens, cotangent, pair, sems):
    rows = pair.shape[1]
    line = pl.ds(pl.multiple_of(place[1] * rows, rows), rows)
    copy_all([(tokens.at[line, :], pair.at[0]), (cotangent.at[line, :], pair.at[1])], sems)


def half_kernel(place, w_in, w_out, keep, send, sems):
    size = keep.shape[1]
    stays_in, goes_in = halves_of(w_in, 1, size, place[2])
    stays_out, goes_out = halves_of(w_out, 0, size, place[2])
    copy_all(
        [
            (goes_in, send.at[0]),
            (goes_out, send.at[1]),
            (stays_in, keep.at[0]),
            (stays_out, keep.at[1]),
        ],
        sems,
    )


def forward_kernel(before, beyond, up, down):
    size = up.shape[0]
    up[...] = before[:size]
    down[...] = beyond[size:]


def pass_kernel(send, out):
    out[...] = send[...]


def stack_kernel(one, two, out):
    out[0] = one[...]
    out[1] = two[...]


def add_kernel(moving, mine, out):
    out[...] = (moving[...].astype(F32) + mine[...].astype(F32)).astype(BF16)


def add_rounded(moving, mine, follows=()):
    return call_kernel(add_kernel, [like(mine)], [moving, mine], follows=follows)[0]


def act_kernel(own, far, near, out):
    sums = own[...].astype(F32) + far[...].astype(F32) + near[...].astype(F32)
    units = sums.shape[1] // 2
    value, slope = gelu_pair(sums[:, :units])
    out[:, :units] = value.astype(BF16)
    out[:, units:] = (sums[:, units:] * slope).astype(BF16)


def put_tokens(place, whole, right, yy, c, block):
    step, width = block.shape
    k = lax.rem(c + NZ - place[0], NZ)
    at = pl.multiple_of((k * NY + yy) * step, step)
    whole[pl.ds(at, step), slice(width, 2 * width) if right else slice(0, width)] = block


def put_whole(place, whole, right, source):
    step = source.shape[0] // (NZ * NY)
    for yy in range(NY):
        for c in range(NZ):
            line = slice((yy * NZ + c) * step, (yy * NZ + c + 1) * step)
            put_tokens(place, whole, right, yy, c, source[line, :])


def put_quarter(place, whole, right, j, source):
    step = source.shape[0] // NZ
    yy = lax.rem(place[1] + j, NY)
    for c in range(NZ):
        line = slice(c * step, (c + 1) * step)
        put_tokens(place, whole, right, yy, c, source[line, :])


def partial_products(whole_in, whole_out, weight_in, weight_out, out):
    rows, both = out[0].shape
    group = NZ // 2
    for first in range(0, NZ, group):
        line = slice(first * rows, (first + group) * rows)
        for whole, weight, over, columns in (
            (whole_in, weight_in, 0, slice(0, both // 2)),
            (whole_out, weight_out, 1, slice(both // 2, both)),
        ):
            product = lax.dot_general(
                whole[line, :],
                weight[...],
                (((1,), (over,)), ((), ())),
                preferred_element_type=F32,
            ).astype(BF16)
            for k in range(group):
                out[first + k][:, columns] = product[k * rows : (k + 1) * rows]


def first_kernel(place, *refs):
    owns, (mine, above, up, down, below), sources = refs[:2], refs[2:7], refs[7:11]
    out, (whole_in, whole_out, weight_in, weight_out) = refs[11:-4], refs[-4:]
    width, hid = sources[0].shape[1:]
    for array, whole in enumerate((whole_in, whole_out)):
        put_whole(place, whole, False, owns[array])
        opposite = up if array == 0 else down
        for j, source in enumerate((mine.at[array], above.at[array], opposite.at[0], below.at[array])):
            put_quarter(place, whole, True, j, source)
    for d in range(2):
        columns = slice(d * width, (d + 1) * width)
        for f in range(2):
            units = slice(f * hid, (f + 1) * hid)
            weight_in[columns, units] = sources[2 * d + f][0]
            weight_out[units, columns] = sources[2 * d + f][1]
    partial_products(whole_in, whole_out, weight_in, weight_out, out)


def second_kernel(place, near, far, weight_in, weight_out, *refs):
    out, wholes = refs[:-2], refs[-2:]
    for array, whole in enumerate(wholes):
        put_whole(place, whole, False, near.at[array])
        put_whole(place, whole, True, far.at[array])
    partial_products(*wholes, weight_in, weight_out, out)


def partial_sums(kernel, place, operands, tokens, width, hid, more=(), follows=()):
    outs = [jax.ShapeDtypeStruct((tokens // NZ, 4 * hid), BF16)] * NZ
    outs += [jax.ShapeDtypeStruct((tokens, 2 * width), BF16)] * 2 + list(more)
    results = call_kernel(kernel, outs, operands, scalars=place, follows=follows)
    return results[:NZ], results[NZ:]


def grad_kernel(scale, tokens_left, *refs):
    chunks, tokens, outs, whole = refs[: 2 * NZ], refs[2 * NZ : 2 * NZ + 2], refs[-3:-1], refs[-1]
    rows, units = chunks[0].shape[0], whole.shape[1]
    half = NZ * rows
    side = slice(units, 2 * units) if tokens_left else slice(0, units)
    for k in range(2 * NZ):
        whole[k * rows : (k + 1) * rows, :] = chunks[k][:, side]
    width, hid = outs[0].shape[1:] if tokens_left else outs[0].shape[:0:-1]
    for d in range(2):
        columns = slice(d * width, (d + 1) * width)
        for f in range(2):
            total = 0.0
            for part in range(2):
                inner = whole[part * half : (part + 1) * half, f * hid : (f + 1) * hid]
                outer = tokens[part][:, columns]
                left, right = (outer, inner) if tokens_left else (inner, outer)
                total += lax.dot_general(
                    left, right, (((0,), (0,)), ((), ())), preferred_element_type=F32
                )
            outs[f][d] = (total * scale).astype(BF16)


def weight_grad(tokens_left, scale, chunks, tokens, follows=()):
    rows, both = chunks[0].shape
    hid, width = both // 4, tokens[0].shape[1] // 2
    tail = (width, hid) if tokens_left else (hid, width)
    outs = [jax.ShapeDtypeStruct((2,) + tail, BF16)] * 2
    scratch = [pltpu.VMEM((2 * NZ * rows, both // 2), BF16)]
    kernel = functools.partial(grad_kernel, scale, tokens_left)
    return call_kernel(kernel, outs, [*chunks, *tokens], scratch, follows=follows)


def back_kernel(place, *refs):
    chunks, weight, outs, (whole, total) = refs[:NZ], refs[NZ], refs[NZ + 1 : -2], refs[-2:]
    rows, units = chunks[0].shape[0], whole.shape[1]
    step = rows // NY
    width = outs[0].shape[2]
    for k in range(NZ):
        whole[k * rows : (k + 1) * rows, :] = chunks[k][:, units:]
    total[...] = lax.dot_general(
        whole[...], weight[...], (((1,), (1,)), ((), ())), preferred_element_type=F32
    ).astype(BF16)
    for j in range(NY):
        yy = lax.rem(place[1] + j, NY)
        for k in range(NZ):
            at = pl.multiple_of((k * NY + yy) * step, step)
            line = slice(k * step, (k + 1) * step)
            for d in range(2):
                outs[j][d, line, :] = total[pl.ds(at, step), d * width : (d + 1) * width]


def token_grad(place, chunks, weight, follows=()):
    rows, both = chunks[0].shape
    width2 = weight.shape[0]
    outs = [jax.ShapeDtypeStruct((2, NZ * rows // NY, width2 // 2), BF16)] * NY
    scratch = [pltpu.VMEM((NZ * rows, both // 2), BF16), pltpu.VMEM((NZ * rows, width2), BF16)]
    return call_kernel(
        back_kernel, outs, [*chunks, weight], scratch, scalars=place, follows=follows
    )


def send_over_y(outs):
    return [outs[0], shift_y(outs[1], 1), shift_y(outs[2], 2), shift_y(outs[3], 3)]


def sum_kernel(*refs):
    terms, outs = refs[:NY], refs[NY:]
    for d in range(2):
        outs[d][...] = sum(term[d].astype(F32) for term in terms).astype(outs[d].dtype)


def place_kernel(place, own, one, two, three, out):
    step = out.shape[0] // NZ
    for k in range(NZ):
        line = slice(k * step, (k + 1) * step)
        total = own[line, :] + one[line, :].astype(F32)
        total += two[line, :].astype(F32) + three[line, :].astype(F32)
        at = pl.multiple_of(lax.rem(place[0] + k, NZ) * step, step)
        out[pl.ds(at, step), :] = total.astype(BF16)


def gelu_pair(pre_act):
    cumulative = 0.5 * (1.0 + jax.scipy.special.erf(pre_act * INV_ROOT2))
    density = jnp.exp(-0.5 * pre_act * pre_act) * INV_ROOT2PI
    return (pre_act * cumulative, cumulative + pre_act * density)


def leave_kernel(kept, moved, out):
    out[...] = (kept[1].astype(F32) + moved[1].astype(F32)).astype(BF16)


def adam_kernel(axis, place, kept, moved, there, first, second, step_dir, new_first, new_second):
    size = there.shape[axis]
    rows = there.shape[0]
    block = rows // ADAM_STEPS
    for local, which in ((True, place[2]), (False, 1 - place[2])):
        start = pl.multiple_of(which * size, size)
        for step in range(ADAM_STEPS):
            line = slice(step * block, (step + 1) * block)
            if local:
                grad = kept[0, line, :].astype(F32) + moved[0, line, :].astype(F32)
            else:
                grad = there[line, :].astype(F32)
            at = (pl.ds(start + step * block, block), slice(None))
            if axis == 1:
                at = (line, pl.ds(start, size))
            first_new = 0.9 * first[at] + 0.1 * grad
            second_new = 0.99 * second[at] + 0.01 * grad * grad
            new_first[at] = first_new
            new_second[at] = second_new
            scaled = second_new * (1.0 / SECOND_FIX)
            scaled = scaled * lax.rsqrt(scaled) + 1e-08
            step_dir[at] = (first_new * (1.0 / FIRST_FIX) / scaled).astype(BF16)


ADAM_STEPS = 4


def adam_step(axis, place, kept, moved, there, first, second, follows=()):
    return call_kernel(
        functools.partial(adam_kernel, axis),
        [like(first, dtype=BF16), like(first), like(first)],
        [kept, moved, there, first, second],
        scalars=place,
        follows=follows,
    )


def reduce_over_z(parts, long_way, before=lambda sums: ()):
    far = parts[4]
    sums = []
    order = (5, 6, 7) if long_way < 0 else (3, 2, 1)
    for k in order:
        far = add_rounded(shift_z(far, long_way), parts[k], before(sums))
        sums.append(far)
    far = shift_z(far, long_way)
    order = (3, 2, 1) if long_way < 0 else (5, 6, 7)
    near = parts[order[0]]
    for k in order[1:]:
        near = add_rounded(shift_z(near, -long_way), parts[k])
    near = shift_z(near, -long_way)
    return (parts[0], far, near), sums


def gather_over_z(chunk, long_way):
    found = [chunk] + [None] * (NZ - 1)
    far = near = chunk
    for step in range(1, 5):
        far = shift_z(far, long_way)
        found[(-long_way * step) % NZ] = far
        if step < 4:
            near = shift_z(near, -long_way)
            found[(long_way * step) % NZ] = near
    return found


def body(normed, out_grad, w_in, w_out, first_in, second_in, first_out, second_out):
    mx = lax.axis_index("mx")
    y = lax.axis_index("my")
    z, x_hi = mx // 2, mx % 2
    place = jnp.stack([z, y, x_hi]).astype(jnp.int32)
    rows = normed.shape[0] // NY
    width, hid = w_in.shape[0], w_in.shape[1] // 2

    (pair,) = copy_kernel(
        quarter_kernel,
        [like(normed, (2, rows, width))],
        place,
        [normed, out_grad],
        2,
        vmem=WHOLE_VMEM_BYTES,
    )
    keep, send = copy_kernel(half_kernel, [like(w_in, (2, width, hid))] * 2, place, [w_in, w_out], 4)
    mine = swap_x_hi(pair)
    (send,) = call_kernel(pass_kernel, [like(send)], [send], follows=[mine])
    part = swap_x_hi(send)
    above, below = shift_y(mine, -1), shift_y(mine, 1)
    up, down = call_kernel(forward_kernel, [like(normed, (1, rows, width))] * 2, [below, above])
    tokens = [mine, above, shift_y(up, 1), shift_y(down, -1), below]
    (part,) = call_kernel(pass_kernel, [like(part)], [part], follows=tokens[2:4])
    weights = [keep, swap_core(keep), part, swap_core(part)]
    count = normed.shape[0]
    parts, (near_in, near_out, weight_in, weight_out) = partial_sums(
        first_kernel,
        place,
        [normed, out_grad, *tokens, *weights],
        count,
        width,
        hid,
        [like(w_in, (2 * width, 2 * hid)), like(w_in, (2 * hid, 2 * width))],
    )
    (sent,) = call_kernel(
        stack_kernel, [like(normed, (2, count, width))], [normed, out_grad], follows=[part]
    )
    beside = [swap_x_lo(sent), swap_x_both(sent)]
    late = []

    def before(sums):
        if len(sums) == 2:
            late.extend(
                partial_sums(
                    second_kernel,
                    place,
                    [*beside, weight_in, weight_out],
                    count,
                    width,
                    hid,
                    follows=sums[1:],
                )
            )
        return [late[0][4]] if late else []

    terms, _ = reduce_over_z(parts, -1, before)
    late_parts, (far_in, far_out) = late
    late_terms, late_sums = reduce_over_z(late_parts, 1)
    chunk = call_kernel(act_kernel, [like(parts[0])], terms, follows=late_sums[:1])[0]
    near_chunks = gather_over_z(chunk, 1)
    chunk = call_kernel(
        act_kernel, [like(parts[0])], late_terms, follows=[near_chunks[2], near_chunks[6]]
    )[0]
    far_chunks = gather_over_z(chunk, -1)

    block = (rows, width)
    sums = send_over_y(token_grad(place, near_chunks, weight_in))
    own, side = call_kernel(sum_kernel, [like(normed, block, F32), like(normed, block)], sums)
    images = float(count * lax.axis_size("dp") // PATCHES)
    chunks = [*near_chunks, *far_chunks]
    kept_out, swapped = weight_grad(False, 1.0 / images, chunks, [near_out, far_out], [side])
    moved_out = swap_core(swapped)
    kept_in, swapped_in = weight_grad(
        True, 1.0 / images, chunks, [near_in, far_in], [kept_out]
    )
    moved_in = swap_core(swapped_in)
    leaving_out = call_kernel(
        leave_kernel, [like(swapped, (hid, width))], [kept_out, moved_out], follows=[kept_in]
    )[0]
    there_out = swap_x_hi(leaving_out)
    late = token_grad(place, far_chunks, weight_in, [leaving_out])
    sums = send_over_y(late)
    leaving_in = call_kernel(
        leave_kernel, [like(swapped_in, (width, hid))], [kept_in, moved_in], follows=late[:1]
    )[0]
    there_in = swap_x_hi(leaving_in)
    other_side, both = call_kernel(sum_kernel, [like(normed, block)] * 2, sums, follows=[leaving_in])
    update_out, new_first_out, new_second_out = adam_step(
        0, place, kept_out, moved_out, there_out, first_out, second_out, [other_side]
    )
    update_in, new_first_in, new_second_in = adam_step(
        1, place, kept_in, moved_in, there_in, first_in, second_in, [update_out]
    )
    input_grad = call_kernel(
        place_kernel,
        [like(normed, block)],
        [own, swap_x_lo(other_side), swap_x_hi(side), swap_x_both(both)],
        scalars=place,
        follows=[update_in],
    )[0]
    return (
        input_grad,
        update_in,
        new_first_in,
        new_second_in,
        update_out,
        new_first_out,
        new_second_out,
    )


def solution(mesh):
    in_specs = (
        P("dp", "mx"),
        P("dp", "mx"),
        P("mx", ("my", "dp")),
        P(("my", "dp"), "mx"),
        P("mx", ("my", "dp")),
        P("mx", ("my", "dp")),
        P(("my", "dp"), "mx"),
        P(("my", "dp"), "mx"),
    )
    out_specs = (
        P(("dp", "my"), "mx"),
        P("mx", ("my", "dp")),
        P("mx", ("my", "dp")),
        P("mx", ("my", "dp")),
        P(("my", "dp"), "mx"),
        P(("my", "dp"), "mx"),
        P(("my", "dp"), "mx"),
    )
    return jax.shard_map(body, mesh=mesh, in_specs=in_specs, out_specs=out_specs, check_vma=False)
```

```python
import functools

import jax
import jax.numpy as jnp
from jax import lax
from jax.experimental import pallas as pl
from jax.experimental.pallas import tpu as pltpu
from jax.sharding import PartitionSpec as P

PATCHES = 256
FREE_SUMS = 1
NZ = 8
NY = 4
INV_ROOT2 = 0.7071067811865476
INV_ROOT2PI = 0.3989422804014327
FIRST_FIX = 1.0 - 0.9**10
SECOND_FIX = 1.0 - 0.99**10
BF16 = jnp.bfloat16
F32 = jnp.float32
VMEM_BYTES = 24 * 1024 * 1024
WHOLE_VMEM_BYTES = 63 * 1024 * 1024


def swap_core(value):
    return lax.ppermute(value, "dp", [(i, i ^ 1) for i in range(4)])


def swap_x_lo(value):
    return lax.ppermute(value, "dp", [(i, i ^ 2) for i in range(4)])


def swap_x_hi(value):
    return lax.ppermute(value, "mx", [(i, i ^ 1) for i in range(16)])


def swap_x_both(value):
    pairs = [(d * 16 + m, (d ^ 2) * 16 + (m ^ 1)) for d in range(4) for m in range(16)]
    return lax.ppermute(value, ("dp", "mx"), pairs)


def shift_z(value, by):
    return lax.ppermute(value, "mx", [(i, (i + 2 * by) % 16) for i in range(16)])


def shift_y(value, by):
    return lax.ppermute(value, "my", [(i, (i + by) % NY) for i in range(NY)])


def vmem_specs(count):
    return [pl.BlockSpec(memory_space=pltpu.VMEM)] * count


def call_kernel(kernel, out_shapes, operands, scratch=(), scalars=None, follows=()):
    operands, follows = list(operands), list(follows)
    moved = sum(o.size * o.dtype.itemsize for o in operands)
    moved += sum(o.size * o.dtype.itemsize for o in out_shapes)
    in_specs = vmem_specs(len(operands))
    in_specs += [pl.BlockSpec(memory_space=pl.ANY)] * len(follows)
    skip, count = len(operands), len(follows)
    operands += follows
    if scalars is not None:
        in_specs = [pl.BlockSpec(memory_space=pltpu.SMEM)] + in_specs
        operands = [scalars] + operands
        skip += 1

    def run(*refs):
        kernel(*refs[:skip], *refs[skip + count :])

    return pl.pallas_call(
        run,
        out_shape=out_shapes,
        in_specs=in_specs,
        out_specs=vmem_specs(len(out_shapes)),
        scratch_shapes=list(scratch),
        compiler_params=pltpu.CompilerParams(vmem_limit_bytes=VMEM_BYTES),
        cost_estimate=pl.CostEstimate(flops=0, bytes_accessed=0, transcendentals=0),
    )(*operands)


def like(array, shape=None, dtype=None):
    return jax.ShapeDtypeStruct(shape or array.shape, dtype or array.dtype)


def copy_all(pairs, sems):
    copies = [pltpu.make_async_copy(src, dst, sems.at[i]) for i, (src, dst) in enumerate(pairs)]
    for copy in copies:
        copy.start()
    for copy in copies:
        copy.wait()


def copy_kernel(kernel, out_shapes, place, operands, copies, follows=(), vmem=VMEM_BYTES):
    count = len(operands)

    def run(place_ref, *refs):
        kernel(place_ref, *refs[:count], *refs[count + len(follows) :])

    return pl.pallas_call(
        run,
        out_shape=out_shapes,
        in_specs=[pl.BlockSpec(memory_space=pltpu.SMEM)]
        + [pl.BlockSpec(memory_space=pltpu.HBM)] * count
        + [pl.BlockSpec(memory_space=pl.ANY)] * len(follows),
        out_specs=vmem_specs(len(out_shapes)),
        scratch_shapes=[pltpu.SemaphoreType.DMA((copies,))],
        compiler_params=pltpu.CompilerParams(vmem_limit_bytes=vmem),
        cost_estimate=pl.CostEstimate(flops=0, bytes_accessed=0, transcendentals=0),
    )(place, *operands, *follows)


def halves_of(weight, axis, size, x_hi):
    views = []
    for which in (x_hi, 1 - x_hi):
        half = pl.ds(pl.multiple_of(which * size, size), size)
        views.append(weight.at[half, :] if axis == 0 else weight.at[:, half])
    return views


def quarter_kernel(place, tokens, cotangent, pair, sems):
    rows = pair.shape[1]
    line = pl.ds(pl.multiple_of(place[1] * rows, rows), rows)
    copy_all([(tokens.at[line, :], pair.at[0]), (cotangent.at[line, :], pair.at[1])], sems)


def half_kernel(place, w_in, w_out, keep, send, sems):
    size = keep.shape[1]
    stays_in, goes_in = halves_of(w_in, 1, size, place[2])
    stays_out, goes_out = halves_of(w_out, 0, size, place[2])
    copy_all(
        [
            (goes_in, send.at[0]),
            (goes_out, send.at[1]),
            (stays_in, keep.at[0]),
            (stays_out, keep.at[1]),
        ],
        sems,
    )


def forward_kernel(before, beyond, up, down):
    size = up.shape[0]
    up[...] = before[:size]
    down[...] = beyond[size:]


def pass_kernel(send, out):
    out[...] = send[...]


def stack_kernel(one, two, out):
    out[0] = one[...]
    out[1] = two[...]


def add_kernel(moving, mine, out):
    out[...] = (moving[...].astype(F32) + mine[...].astype(F32)).astype(BF16)


def add_rounded(moving, mine, follows=()):
    return call_kernel(add_kernel, [like(mine)], [moving, mine], follows=follows)[0]


def act_kernel(own, far, near, out):
    sums = own[...].astype(F32) + far[...].astype(F32) + near[...].astype(F32)
    units = sums.shape[1] // 2
    value, slope = gelu_pair(sums[:, :units])
    out[:, :units] = value.astype(BF16)
    out[:, units:] = (sums[:, units:] * slope).astype(BF16)


def put_tokens(place, whole, right, yy, c, block):
    step, width = block.shape
    k = lax.rem(c + NZ - place[0], NZ)
    at = pl.multiple_of((k * NY + yy) * step, step)
    whole[pl.ds(at, step), slice(width, 2 * width) if right else slice(0, width)] = block


def put_whole(place, whole, right, source):
    step = source.shape[0] // (NZ * NY)
    for yy in range(NY):
        for c in range(NZ):
            line = slice((yy * NZ + c) * step, (yy * NZ + c + 1) * step)
            put_tokens(place, whole, right, yy, c, source[line, :])


def put_quarter(place, whole, right, j, source):
    step = source.shape[0] // NZ
    yy = lax.rem(place[1] + j, NY)
    for c in range(NZ):
        line = slice(c * step, (c + 1) * step)
        put_tokens(place, whole, right, yy, c, source[line, :])


def partial_products(whole_in, whole_out, weight_in, weight_out, out):
    rows, both = out[0].shape
    group = NZ // 2
    for first in range(0, NZ, group):
        line = slice(first * rows, (first + group) * rows)
        for whole, weight, over, columns in (
            (whole_in, weight_in, 0, slice(0, both // 2)),
            (whole_out, weight_out, 1, slice(both // 2, both)),
        ):
            product = lax.dot_general(
                whole[line, :],
                weight[...],
                (((1,), (over,)), ((), ())),
                preferred_element_type=F32,
            ).astype(BF16)
            for k in range(group):
                out[first + k][:, columns] = product[k * rows : (k + 1) * rows]


def first_kernel(place, *refs):
    owns, (mine, above, up, down, below), sources = refs[:2], refs[2:7], refs[7:11]
    out, (whole_in, whole_out, weight_in, weight_out) = refs[11:-4], refs[-4:]
    width, hid = sources[0].shape[1:]
    for array, whole in enumerate((whole_in, whole_out)):
        put_whole(place, whole, False, owns[array])
        opposite = up if array == 0 else down
        for j, source in enumerate((mine.at[array], above.at[array], opposite.at[0], below.at[array])):
            put_quarter(place, whole, True, j, source)
    for d in range(2):
        columns = slice(d * width, (d + 1) * width)
        for f in range(2):
            units = slice(f * hid, (f + 1) * hid)
            weight_in[columns, units] = sources[2 * d + f][0]
            weight_out[units, columns] = sources[2 * d + f][1]
    partial_products(whole_in, whole_out, weight_in, weight_out, out)


def second_kernel(place, near, far, weight_in, weight_out, *refs):
    out, wholes = refs[:-2], refs[-2:]
    for array, whole in enumerate(wholes):
        put_whole(place, whole, False, near.at[array])
        put_whole(place, whole, True, far.at[array])
    partial_products(*wholes, weight_in, weight_out, out)


def partial_sums(kernel, place, operands, tokens, width, hid, more=(), follows=()):
    outs = [jax.ShapeDtypeStruct((tokens // NZ, 4 * hid), BF16)] * NZ
    outs += [jax.ShapeDtypeStruct((tokens, 2 * width), BF16)] * 2 + list(more)
    results = call_kernel(kernel, outs, operands, scalars=place, follows=follows)
    return results[:NZ], results[NZ:]


def grad_kernel(scale, tokens_left, *refs):
    chunks, tokens, outs, whole = refs[: 2 * NZ], refs[2 * NZ : 2 * NZ + 2], refs[-3:-1], refs[-1]
    rows, units = chunks[0].shape[0], whole.shape[1]
    half = NZ * rows
    side = slice(units, 2 * units) if tokens_left else slice(0, units)
    for k in range(2 * NZ):
        whole[k * rows : (k + 1) * rows, :] = chunks[k][:, side]
    width, hid = outs[0].shape[1:] if tokens_left else outs[0].shape[:0:-1]
    for d in range(2):
        columns = slice(d * width, (d + 1) * width)
        for f in range(2):
            total = 0.0
            for part in range(2):
                inner = whole[part * half : (part + 1) * half, f * hid : (f + 1) * hid]
                outer = tokens[part][:, columns]
                left, right = (outer, inner) if tokens_left else (inner, outer)
                total += lax.dot_general(
                    left, right, (((0,), (0,)), ((), ())), preferred_element_type=F32
                )
            outs[f][d] = (total * scale).astype(BF16)


def weight_grad(tokens_left, scale, chunks, tokens, follows=()):
    rows, both = chunks[0].shape
    hid, width = both // 4, tokens[0].shape[1] // 2
    tail = (width, hid) if tokens_left else (hid, width)
    outs = [jax.ShapeDtypeStruct((2,) + tail, BF16)] * 2
    scratch = [pltpu.VMEM((2 * NZ * rows, both // 2), BF16)]
    kernel = functools.partial(grad_kernel, scale, tokens_left)
    return call_kernel(kernel, outs, [*chunks, *tokens], scratch, follows=follows)


def back_kernel(place, *refs):
    chunks, weight, outs, (whole, total) = refs[:NZ], refs[NZ], refs[NZ + 1 : -2], refs[-2:]
    rows, units = chunks[0].shape[0], whole.shape[1]
    step = rows // NY
    width = outs[0].shape[2]
    for k in range(NZ):
        whole[k * rows : (k + 1) * rows, :] = chunks[k][:, units:]
    total[...] = lax.dot_general(
        whole[...], weight[...], (((1,), (1,)), ((), ())), preferred_element_type=F32
    ).astype(BF16)
    for j in range(NY):
        yy = lax.rem(place[1] + j, NY)
        for k in range(NZ):
            at = pl.multiple_of((k * NY + yy) * step, step)
            line = slice(k * step, (k + 1) * step)
            for d in range(2):
                outs[j][d, line, :] = total[pl.ds(at, step), d * width : (d + 1) * width]


def token_grad(place, chunks, weight, follows=()):
    rows, both = chunks[0].shape
    width2 = weight.shape[0]
    outs = [jax.ShapeDtypeStruct((2, NZ * rows // NY, width2 // 2), BF16)] * NY
    scratch = [pltpu.VMEM((NZ * rows, both // 2), BF16), pltpu.VMEM((NZ * rows, width2), BF16)]
    return call_kernel(
        back_kernel, outs, [*chunks, weight], scratch, scalars=place, follows=follows
    )


def send_over_y(outs):
    return [outs[0], shift_y(outs[1], 1), shift_y(outs[2], 2), shift_y(outs[3], 3)]


def sum_kernel(*refs):
    terms, outs = refs[:NY], refs[NY:]
    for d in range(2):
        outs[d][...] = sum(term[d].astype(F32) for term in terms).astype(outs[d].dtype)


def place_kernel(place, own, one, two, three, out):
    step = out.shape[0] // NZ
    for k in range(NZ):
        line = slice(k * step, (k + 1) * step)
        total = own[line, :] + one[line, :].astype(F32)
        total += two[line, :].astype(F32) + three[line, :].astype(F32)
        at = pl.multiple_of(lax.rem(place[0] + k, NZ) * step, step)
        out[pl.ds(at, step), :] = total.astype(BF16)


def gelu_pair(pre_act):
    cumulative = 0.5 * (1.0 + jax.scipy.special.erf(pre_act * INV_ROOT2))
    density = jnp.exp(-0.5 * pre_act * pre_act) * INV_ROOT2PI
    return (pre_act * cumulative, cumulative + pre_act * density)


def leave_kernel(kept, moved, out):
    out[...] = (kept[1].astype(F32) + moved[1].astype(F32)).astype(BF16)


def adam_kernel(axis, place, kept, moved, there, first, second, step_dir, new_first, new_second, mark):
    mark[...] = jnp.zeros_like(mark)
    size = there.shape[axis]
    rows = there.shape[0]
    block = rows // ADAM_STEPS
    for local, which in ((True, place[2]), (False, 1 - place[2])):
        start = pl.multiple_of(which * size, size)
        for step in range(ADAM_STEPS):
            line = slice(step * block, (step + 1) * block)
            if local:
                grad = kept[0, line, :].astype(F32) + moved[0, line, :].astype(F32)
            else:
                grad = there[line, :].astype(F32)
            at = (pl.ds(start + step * block, block), slice(None))
            if axis == 1:
                at = (line, pl.ds(start, size))
            first_new = 0.9 * first[at] + 0.1 * grad
            second_new = 0.99 * second[at] + 0.01 * grad * grad
            new_first[at] = first_new
            new_second[at] = second_new
            scaled = second_new * (1.0 / SECOND_FIX)
            scaled = scaled * lax.rsqrt(scaled) + 1e-08
            step_dir[at] = (first_new * (1.0 / FIRST_FIX) / scaled).astype(BF16)


ADAM_STEPS = 4


def adam_step(axis, place, kept, moved, there, first, second, follows=()):
    return call_kernel(
        functools.partial(adam_kernel, axis),
        [like(first, dtype=BF16), like(first), like(first), like(first, (8, 128))],
        [kept, moved, there, first, second],
        scalars=place,
        follows=follows,
    )


def reduce_over_z(parts, long_way, before=lambda sums: ()):
    far = parts[4]
    sums = []
    order = (5, 6, 7) if long_way < 0 else (3, 2, 1)
    for k in order:
        far = add_rounded(shift_z(far, long_way), parts[k], before(sums))
        sums.append(far)
    far = shift_z(far, long_way)
    order = (3, 2, 1) if long_way < 0 else (5, 6, 7)
    near = parts[order[0]]
    for k in order[1:]:
        near = add_rounded(shift_z(near, -long_way), parts[k])
    near = shift_z(near, -long_way)
    return (parts[0], far, near), sums


def gather_over_z(chunk, long_way):
    found = [chunk] + [None] * (NZ - 1)
    far = near = chunk
    for step in range(1, 5):
        far = shift_z(far, long_way)
        found[(-long_way * step) % NZ] = far
        if step < 4:
            near = shift_z(near, -long_way)
            found[(long_way * step) % NZ] = near
    return found


def body(normed, out_grad, w_in, w_out, first_in, second_in, first_out, second_out):
    mx = lax.axis_index("mx")
    y = lax.axis_index("my")
    z, x_hi = mx // 2, mx % 2
    place = jnp.stack([z, y, x_hi]).astype(jnp.int32)
    count = normed.shape[0]
    rows = count // NY
    width, hid = w_in.shape[0], w_in.shape[1] // 2

    (pair,) = copy_kernel(
        quarter_kernel,
        [like(normed, (2, rows, width))],
        place,
        [normed, out_grad],
        2,
        vmem=WHOLE_VMEM_BYTES,
    )
    keep, send = copy_kernel(half_kernel, [like(w_in, (2, width, hid))] * 2, place, [w_in, w_out], 4)
    mine = swap_x_hi(pair)
    (send,) = call_kernel(pass_kernel, [like(send)], [send], follows=[mine])
    part = swap_x_hi(send)
    above, below = shift_y(mine, -1), shift_y(mine, 1)
    other = swap_core(keep)
    up, down = call_kernel(
        forward_kernel, [like(normed, (1, rows, width))] * 2, [below, above], follows=[other]
    )
    tokens = [mine, above, shift_y(up, 1), shift_y(down, -1), below]
    (sent,) = call_kernel(
        stack_kernel, [like(normed, (2, count, width))], [normed, out_grad], follows=[up]
    )
    (part,) = call_kernel(pass_kernel, [like(part)], [part], follows=[*tokens[2:4], sent])
    weights = [keep, other, part, swap_core(part)]
    parts, (near_in, near_out, weight_in, weight_out) = partial_sums(
        first_kernel,
        place,
        [normed, out_grad, *tokens, *weights],
        count,
        width,
        hid,
        [like(w_in, (2 * width, 2 * hid)), like(w_in, (2 * hid, 2 * width))],
    )
    beside = [swap_x_lo(sent), swap_x_both(sent)]
    late = []

    def before(sums):
        if len(sums) == FREE_SUMS:
            late.extend(
                partial_sums(
                    second_kernel,
                    place,
                    [*beside, weight_in, weight_out],
                    count,
                    width,
                    hid,
                    follows=sums[FREE_SUMS - 1 : FREE_SUMS],
                )
            )
        return [late[0][4]] if len(sums) == 2 else []

    terms, _ = reduce_over_z(parts, -1, before)
    late_parts, (far_in, far_out) = late
    late_terms, late_sums = reduce_over_z(late_parts, 1)
    chunk = call_kernel(act_kernel, [like(parts[0])], terms, follows=late_sums[:1])[0]
    near_chunks = gather_over_z(chunk, 1)
    chunk = call_kernel(
        act_kernel, [like(parts[0])], late_terms, follows=[near_chunks[1], near_chunks[7]]
    )[0]
    far_chunks = gather_over_z(chunk, -1)

    block = (rows, width)
    sums = send_over_y(token_grad(place, near_chunks, weight_in))
    own, side = call_kernel(sum_kernel, [like(normed, block, F32), like(normed, block)], sums)
    images = float(count * lax.axis_size("dp") // PATCHES)
    chunks = [*near_chunks, *far_chunks]
    kept_out, swapped = weight_grad(False, 1.0 / images, chunks, [near_out, far_out], [side])
    moved_out = swap_core(swapped)
    late = token_grad(place, far_chunks, weight_in, [kept_out])
    leaving_out = call_kernel(
        leave_kernel, [like(swapped, (hid, width))], [kept_out, moved_out], follows=late[:1]
    )[0]
    there_out = swap_x_hi(leaving_out)
    sums = send_over_y(late)
    kept_in, swapped = weight_grad(
        True, 1.0 / images, chunks, [near_in, far_in], [leaving_out]
    )
    moved_in = swap_core(swapped)
    leaving_in = call_kernel(
        leave_kernel, [like(swapped, (width, hid))], [kept_in, moved_in]
    )[0]
    there_in = swap_x_hi(leaving_in)
    update_out, new_first_out, new_second_out, mark = adam_step(
        0, place, kept_out, moved_out, there_out, first_out, second_out, [leaving_in]
    )
    other_side, both = call_kernel(sum_kernel, [like(normed, block)] * 2, sums, follows=[mark])
    update_in, new_first_in, new_second_in, mark = adam_step(
        1, place, kept_in, moved_in, there_in, first_in, second_in, [other_side]
    )
    input_grad = call_kernel(
        place_kernel,
        [like(normed, block)],
        [own, swap_x_lo(other_side), swap_x_hi(side), swap_x_both(both)],
        scalars=place,
        follows=[mark],
    )[0]
    return (
        input_grad,
        update_in,
        new_first_in,
        new_second_in,
        update_out,
        new_first_out,
        new_second_out,
    )


def solution(mesh):
    in_specs = (
        P("dp", "mx"),
        P("dp", "mx"),
        P("mx", ("my", "dp")),
        P(("my", "dp"), "mx"),
        P("mx", ("my", "dp")),
        P("mx", ("my", "dp")),
        P(("my", "dp"), "mx"),
        P(("my", "dp"), "mx"),
    )
    out_specs = (
        P(("dp", "my"), "mx"),
        P("mx", ("my", "dp")),
        P("mx", ("my", "dp")),
        P("mx", ("my", "dp")),
        P(("my", "dp"), "mx"),
        P(("my", "dp"), "mx"),
        P(("my", "dp"), "mx"),
    )
    return jax.shard_map(body, mesh=mesh, in_specs=in_specs, out_specs=out_specs, check_vma=False)
```

```python
import functools

import jax
import jax.numpy as jnp
from jax import lax
from jax.experimental import pallas as pl
from jax.experimental.pallas import tpu as pltpu
from jax.sharding import PartitionSpec as P

PATCHES = 256
NZ = 8
NY = 4
INV_ROOT2 = 0.7071067811865476
INV_ROOT2PI = 0.3989422804014327
FIRST_FIX = 1.0 - 0.9**10
SECOND_FIX = 1.0 - 0.99**10
BF16 = jnp.bfloat16
F32 = jnp.float32
VMEM_BYTES = 24 * 1024 * 1024
WHOLE_VMEM_BYTES = 63 * 1024 * 1024


def swap_core(value):
    return lax.ppermute(value, "dp", [(i, i ^ 1) for i in range(4)])


def swap_x_lo(value):
    return lax.ppermute(value, "dp", [(i, i ^ 2) for i in range(4)])


def swap_x_hi(value):
    return lax.ppermute(value, "mx", [(i, i ^ 1) for i in range(16)])


def swap_x_both(value):
    pairs = [(d * 16 + m, (d ^ 2) * 16 + (m ^ 1)) for d in range(4) for m in range(16)]
    return lax.ppermute(value, ("dp", "mx"), pairs)


def shift_z(value, by):
    return lax.ppermute(value, "mx", [(i, (i + 2 * by) % 16) for i in range(16)])


def shift_y(value, by):
    return lax.ppermute(value, "my", [(i, (i + by) % NY) for i in range(NY)])


def vmem_specs(count):
    return [pl.BlockSpec(memory_space=pltpu.VMEM)] * count


def call_kernel(kernel, out_shapes, operands, scratch=(), flops=0, scalars=None, follows=()):
    operands, follows = list(operands), list(follows)
    moved = sum(o.size * o.dtype.itemsize for o in operands)
    moved += sum(o.size * o.dtype.itemsize for o in out_shapes)
    in_specs = vmem_specs(len(operands))
    in_specs += [pl.BlockSpec(memory_space=pl.ANY)] * len(follows)
    skip, count = len(operands), len(follows)
    operands += follows
    if scalars is not None:
        in_specs = [pl.BlockSpec(memory_space=pltpu.SMEM)] + in_specs
        operands = [scalars] + operands
        skip += 1

    def run(*refs):
        kernel(*refs[:skip], *refs[skip + count :])

    return pl.pallas_call(
        run,
        out_shape=out_shapes,
        in_specs=in_specs,
        out_specs=vmem_specs(len(out_shapes)),
        scratch_shapes=list(scratch),
        compiler_params=pltpu.CompilerParams(vmem_limit_bytes=VMEM_BYTES),
        cost_estimate=pl.CostEstimate(flops=0, bytes_accessed=0, transcendentals=0),
    )(*operands)


def like(array, shape=None, dtype=None):
    return jax.ShapeDtypeStruct(shape or array.shape, dtype or array.dtype)


def copy_all(pairs, sems):
    copies = [pltpu.make_async_copy(src, dst, sems.at[i]) for i, (src, dst) in enumerate(pairs)]
    for copy in copies:
        copy.start()
    for copy in copies:
        copy.wait()


def copy_kernel(kernel, out_shapes, place, operands, copies, follows=(), vmem=VMEM_BYTES):
    count = len(operands)

    def run(place_ref, *refs):
        kernel(place_ref, *refs[:count], *refs[count + len(follows) :])

    return pl.pallas_call(
        run,
        out_shape=out_shapes,
        in_specs=[pl.BlockSpec(memory_space=pltpu.SMEM)]
        + [pl.BlockSpec(memory_space=pltpu.HBM)] * count
        + [pl.BlockSpec(memory_space=pl.ANY)] * len(follows),
        out_specs=vmem_specs(len(out_shapes)),
        scratch_shapes=[pltpu.SemaphoreType.DMA((copies,))],
        compiler_params=pltpu.CompilerParams(vmem_limit_bytes=vmem),
        cost_estimate=pl.CostEstimate(flops=0, bytes_accessed=0, transcendentals=0),
    )(place, *operands, *follows)


def halves_of(weight, axis, size, x_hi):
    views = []
    for which in (x_hi, 1 - x_hi):
        half = pl.ds(pl.multiple_of(which * size, size), size)
        views.append(weight.at[half, :] if axis == 0 else weight.at[:, half])
    return views


def quarter_kernel(place, tokens, cotangent, pair, sems):
    rows = pair.shape[1]
    line = pl.ds(pl.multiple_of(place[1] * rows, rows), rows)
    copy_all([(tokens.at[line, :], pair.at[0]), (cotangent.at[line, :], pair.at[1])], sems)


def half_kernel(place, w_in, w_out, keep, send, sems):
    size = keep.shape[1]
    stays_in, goes_in = halves_of(w_in, 1, size, place[2])
    stays_out, goes_out = halves_of(w_out, 0, size, place[2])
    copy_all(
        [
            (goes_in, send.at[0]),
            (goes_out, send.at[1]),
            (stays_in, keep.at[0]),
            (stays_out, keep.at[1]),
        ],
        sems,
    )


def forward_kernel(before, beyond, up, down):
    size = up.shape[0]
    up[...] = before[:size]
    down[...] = beyond[size:]


def stack_kernel(one, two, three, send, out, passed):
    for array in range(2):
        for p, source in enumerate((one, two, three)):
            out[3 * array + p] = source[array]
    passed[...] = send[...]


def add_kernel(moving, mine, out):
    out[...] = (moving[...].astype(F32) + mine[...].astype(F32)).astype(BF16)


def add_rounded(moving, mine, follows=()):
    return call_kernel(add_kernel, [like(mine)], [moving, mine], follows=follows)[0]


def act_kernel(own, far, near, act, slope):
    pre_act = own[...].astype(F32) + far[...].astype(F32) + near[...].astype(F32)
    value, slope[...] = gelu_pair(pre_act)
    act[...] = value.astype(BF16)


def act_grad_kernel(own, far, near, slope, out):
    act_back = own[...].astype(F32) + far[...].astype(F32) + near[...].astype(F32)
    out[...] = (act_back * slope[...]).astype(BF16)


def assemble_tokens(place, own, moved, first, whole, rows, width):
    z, y = place[0], place[1]
    step = rows // NZ

    def put(c, side, yy, right, block):
        k = lax.rem(c + NZ - z, NZ)
        at = pl.multiple_of(((k * 2 + side) * NY + yy) * step, step)
        columns = slice(width, 2 * width) if right else slice(0, width)
        whole[pl.ds(at, step), columns] = block

    for c in range(NZ):
        for yy in range(NY):
            put(c, 0, yy, False, own[yy * rows + c * step : yy * rows + (c + 1) * step, :])
        line = slice(c * step, (c + 1) * step)
        for j in range(NY):
            yy = lax.rem(y + j, NY)
            skip = 0 if moved[j].shape[0] == 3 else first
            put(c, 1, yy, False, moved[j][skip, line, :])
            put(c, 1, yy, True, moved[j][skip + 1, line, :])
            put(c, 0, yy, True, moved[j][skip + 2, line, :])


def partial_kernel(by_rows, place, own, *refs):
    moved, sources = refs[:NY], refs[NY : NY + 4]
    out, (whole, weight) = refs[NY + 4 : -2], refs[-2:]
    which = 0 if by_rows else 1
    rows, width = own.shape[0] // NY, own.shape[1]
    hid = sources[0].shape[2] if by_rows else sources[0].shape[1]
    assemble_tokens(place, own, moved, 3 * which, whole, rows, width)
    for d in range(2):
        columns = slice(d * width, (d + 1) * width)
        for f in range(2):
            units = slice(f * hid, (f + 1) * hid)
            weight[(columns, units) if by_rows else (units, columns)] = sources[2 * d + f][which]
    contract = (((1,), (0,)), ((), ())) if by_rows else (((1,), (1,)), ((), ()))
    for k in range(0, NZ, 2):
        rows_k = slice(k * rows, (k + 2) * rows)
        both = lax.dot_general(whole[rows_k, :], weight[...], contract, preferred_element_type=F32)
        out[k][...] = both[:rows].astype(BF16)
        out[k + 1][...] = both[rows:].astype(BF16)


def partial_sums(by_rows, place, own, moved, weights, follows=()):
    rows, width = own.shape[0] // NY, own.shape[1]
    hid = weights[0].shape[2 if by_rows else 1]
    outs = [jax.ShapeDtypeStruct((rows, 2 * hid), BF16)] * NZ + [
        jax.ShapeDtypeStruct((NZ * rows, 2 * width), BF16),
        jax.ShapeDtypeStruct((2 * width, 2 * hid) if by_rows else (2 * hid, 2 * width), BF16),
    ]
    flops = 2 * NZ * rows * 2 * width * 2 * hid

    def kernel(*refs):
        partial_kernel(by_rows, *refs)

    results = call_kernel(kernel, outs, [own, *moved, *weights], [], flops, place, follows)
    return results[:NZ], results[NZ], results[NZ + 1]


def grad_kernel(scale, tokens_left, *refs):
    chunks, tokens, outs, whole = refs[:NZ], refs[NZ], refs[NZ + 1 : NZ + 3], refs[NZ + 3]
    rows = chunks[0].shape[0]
    for k in range(NZ):
        whole[k * rows : (k + 1) * rows, :] = chunks[k][...]
    width, hid = outs[0].shape[1:] if tokens_left else outs[0].shape[:0:-1]
    over = (((0,), (0,)), ((), ()))
    for d in range(2):
        for f in range(2):
            units = whole[:, f * hid : (f + 1) * hid]
            columns = tokens[:, d * width : (d + 1) * width]
            left, right = (columns, units) if tokens_left else (units, columns)
            total = lax.dot_general(left, right, over, preferred_element_type=F32)
            outs[f][d] = (total * scale).astype(BF16)


def weight_grad(tokens_left, scale, chunks, tokens, follows=()):
    rows, hid2 = chunks[0].shape
    width2 = tokens.shape[1]
    hid, width = hid2 // 2, width2 // 2
    tail = (width, hid) if tokens_left else (hid, width)
    outs = [jax.ShapeDtypeStruct((2,) + tail, BF16)] * 2
    flops = 2 * NZ * rows * hid2 * width2

    def kernel(*refs):
        grad_kernel(scale, tokens_left, *refs)

    scratch = [pltpu.VMEM((NZ * rows, hid2), BF16)]
    return call_kernel(kernel, outs, [*chunks, tokens], scratch, flops, follows=follows)


def back_kernel(count, place, *refs):
    chunks, weight = refs[:count], refs[count]
    outs, whole, total = refs[count + 1 : count + 1 + NY], refs[-2], refs[-1]
    y = place[1]
    rows = chunks[0].shape[0]
    step = rows // NZ
    width = outs[0].shape[3]
    for k in range(count):
        whole[k * rows : (k + 1) * rows, :] = chunks[k][...]
    total[...] = lax.dot_general(
        whole[...], weight[...], (((1,), (1,)), ((), ())), preferred_element_type=F32
    ).astype(BF16)
    for j in range(NY):
        yy = lax.rem(y + j, NY)
        for k in range(count):
            for side in range(2):
                at = pl.multiple_of(((k * 2 + side) * NY + yy) * step, step)
                line = slice(k * step, (k + 1) * step)
                for d in range(2):
                    columns = slice(d * width, (d + 1) * width)
                    outs[j][side, d, line, :] = total[pl.ds(at, step), columns]


def token_grad(place, chunks, weight, follows=()):
    count = len(chunks)
    rows, hid2 = chunks[0].shape
    width2 = weight.shape[0]
    outs = [jax.ShapeDtypeStruct((2, 2, count * rows // NZ, width2 // 2), BF16)] * NY
    flops = 2 * count * rows * hid2 * width2
    scratch = [pltpu.VMEM((count * rows, hid2), BF16), pltpu.VMEM((count * rows, width2), BF16)]

    def kernel(*refs):
        back_kernel(count, *refs)

    return call_kernel(kernel, outs, [*chunks, weight], scratch, flops, place, follows)


def send_over_y(outs):
    return [outs[0], shift_y(outs[1], 1), shift_y(outs[2], 2), shift_y(outs[3], 3)]


def sum_kernel(*refs):
    terms, outs = refs[:-4], refs[-4:]
    at = 0
    for group in (terms[:NY], terms[NY:]):
        size = group[0].shape[2]
        for side in range(2):
            for d in range(2):
                total = sum(term[side, d].astype(F32) for term in group)
                out = outs[side * 2 + d]
                out[at : at + size, :] = total.astype(out.dtype)
        at += size


def place_kernel(order, place, own, one, two, three, out):
    z = place[0]
    step = out.shape[0] // NZ
    for i, k in enumerate(order):
        line = slice(i * step, (i + 1) * step)
        total = own[line, :] + one[line, :].astype(F32)
        total += two[line, :].astype(F32) + three[line, :].astype(F32)
        at = pl.multiple_of(lax.rem(z + k, NZ) * step, step)
        out[pl.ds(at, step), :] = total.astype(BF16)


def gelu_pair(pre_act):
    cumulative = 0.5 * (1.0 + jax.scipy.special.erf(pre_act * INV_ROOT2))
    density = jnp.exp(-0.5 * pre_act * pre_act) * INV_ROOT2PI
    return (pre_act * cumulative, cumulative + pre_act * density)


def leave_kernel(kept, moved, out):
    out[...] = (kept[1].astype(F32) + moved[1].astype(F32)).astype(BF16)


def adam_kernel(axis, place, kept, moved, there, first, second, step_dir, new_first, new_second, mark):
    mark[...] = jnp.zeros_like(mark)
    size = there.shape[axis]
    rows = there.shape[0]
    block = rows // ADAM_STEPS
    for local, which in ((True, place[2]), (False, 1 - place[2])):
        start = pl.multiple_of(which * size, size)
        for step in range(ADAM_STEPS):
            line = slice(step * block, (step + 1) * block)
            if local:
                grad = kept[0, line, :].astype(F32) + moved[0, line, :].astype(F32)
            else:
                grad = there[line, :].astype(F32)
            at = (pl.ds(start + step * block, block), slice(None))
            if axis == 1:
                at = (line, pl.ds(start, size))
            first_new = 0.9 * first[at] + 0.1 * grad
            second_new = 0.99 * second[at] + 0.01 * grad * grad
            new_first[at] = first_new
            new_second[at] = second_new
            scaled = second_new * (1.0 / SECOND_FIX)
            scaled = scaled * lax.rsqrt(scaled) + 1e-08
            step_dir[at] = (first_new * (1.0 / FIRST_FIX) / scaled).astype(BF16)


ADAM_STEPS = 4


def adam_step(axis, place, kept, moved, there, first, second, follows=()):
    return call_kernel(
        functools.partial(adam_kernel, axis),
        [like(first, dtype=BF16), like(first), like(first), like(first, (8, 128))],
        [kept, moved, there, first, second],
        scalars=place,
        follows=follows,
    )


def reduce_over_z(parts, long_way, follows=()):
    far = parts[4]
    sums = []
    order = (5, 6, 7) if long_way < 0 else (3, 2, 1)
    for i, k in enumerate(order):
        far = add_rounded(shift_z(far, long_way), parts[k], [f for f in follows[i : i + 1] if f is not None])
        sums.append(far)
    far = shift_z(far, long_way)
    order = (3, 2, 1) if long_way < 0 else (5, 6, 7)
    near = parts[order[0]]
    for k in order[1:]:
        near = add_rounded(shift_z(near, -long_way), parts[k])
    near = shift_z(near, -long_way)
    return (parts[0], far, near), sums


def gather_over_z(chunk, long_way):
    found = [chunk] + [None] * (NZ - 1)
    far = near = chunk
    for step in range(1, 5):
        far = shift_z(far, long_way)
        found[(-long_way * step) % NZ] = far
        if step < 4:
            near = shift_z(near, -long_way)
            found[(long_way * step) % NZ] = near
    return found


def body(normed, out_grad, w_in, w_out, first_in, second_in, first_out, second_out):
    mx = lax.axis_index("mx")
    y = lax.axis_index("my")
    z, x_hi = mx // 2, mx % 2
    place = jnp.stack([z, y, x_hi]).astype(jnp.int32)
    rows = normed.shape[0] // NY
    width, hid = w_in.shape[0], w_in.shape[1] // 2

    (pair,) = copy_kernel(
        quarter_kernel,
        [like(normed, (2, rows, width))],
        place,
        [normed, out_grad],
        2,
        vmem=WHOLE_VMEM_BYTES,
    )
    keep, send = copy_kernel(half_kernel, [like(w_in, (2, width, hid))] * 2, place, [w_in, w_out], 4)
    mine, send = call_kernel(
        stack_kernel,
        [like(normed, (6, rows, width)), like(send)],
        [swap_x_lo(pair), swap_x_both(pair), swap_x_hi(pair), send],
    )
    part = swap_x_hi(send)
    above, below = shift_y(mine, -1), shift_y(mine, 1)
    up, down = call_kernel(
        forward_kernel, [like(normed, (3, rows, width))] * 2, [below, above]
    )
    weights = [keep, swap_core(keep), part, swap_core(part)]
    pre_parts, whole_in, weight_in = partial_sums(
        True, place, normed, [mine, above, shift_y(up, 1), below], weights
    )
    back_parts, whole_out, _ = partial_sums(
        False, place, out_grad, [mine, above, shift_y(down, -1), below], weights, [pre_parts[4]]
    )
    back_terms, back_sums = reduce_over_z(back_parts, 1)
    pre_terms, _ = reduce_over_z(pre_parts, -1, [None, back_parts[4], back_sums[0]])
    chunk = pre_parts[0]
    act, slope = call_kernel(act_kernel, [like(chunk), like(chunk, dtype=F32)], pre_terms, follows=back_sums[1:2])
    acts = gather_over_z(act, 1)
    act_grad = call_kernel(act_grad_kernel, [like(chunk)], [*back_terms, slope])[0]
    act_grads = gather_over_z(act_grad, -1)

    images = float(normed.shape[0] * lax.axis_size("dp") // PATCHES)
    first_places, last_places = (0, 1, 7, 2, 6), (3, 5, 4)
    early = token_grad(place, [act_grads[k] for k in first_places], weight_in)
    terms = send_over_y(early)
    kept_out, swapped = weight_grad(False, 1.0 / images, acts, whole_out, terms[1:])
    moved_out = swap_core(swapped)
    kept_in, swapped = weight_grad(True, 1.0 / images, act_grads, whole_in)
    moved_in = swap_core(swapped)
    late = token_grad(
        place, [act_grads[k] for k in last_places], weight_in, [kept_in]
    )
    terms += send_over_y(late)
    leaving_out = call_kernel(
        leave_kernel, [like(w_out, (hid, width))], [kept_out, moved_out], follows=late[:1]
    )[0]
    there_out = swap_x_hi(leaving_out)
    leaving_in = call_kernel(
        leave_kernel, [like(swapped, (width, hid))], [kept_in, moved_in], follows=[leaving_out]
    )[0]
    there_in = swap_x_hi(leaving_in)
    block = (rows, width)
    own, side, other_side, both = call_kernel(
        sum_kernel, [like(normed, block, F32)] + [like(normed, block)] * 3, terms
    )
    update_out, new_first_out, new_second_out, mark = adam_step(
        0, place, kept_out, moved_out, there_out, first_out, second_out, [own]
    )
    update_in, new_first_in, new_second_in, mark = adam_step(
        1, place, kept_in, moved_in, there_in, first_in, second_in, [mark]
    )
    input_grad = call_kernel(
        functools.partial(place_kernel, first_places + last_places),
        [like(normed, block)],
        [own, swap_x_lo(other_side), swap_x_hi(side), swap_x_both(both)],
        scalars=place,
        follows=[mark],
    )[0]
    return (
        input_grad,
        update_in,
        new_first_in,
        new_second_in,
        update_out,
        new_first_out,
        new_second_out,
    )


def solution(mesh):
    in_specs = (
        P("dp", "mx"),
        P("dp", "mx"),
        P("mx", ("my", "dp")),
        P(("my", "dp"), "mx"),
        P("mx", ("my", "dp")),
        P("mx", ("my", "dp")),
        P(("my", "dp"), "mx"),
        P(("my", "dp"), "mx"),
    )
    out_specs = (
        P(("dp", "my"), "mx"),
        P("mx", ("my", "dp")),
        P("mx", ("my", "dp")),
        P("mx", ("my", "dp")),
        P(("my", "dp"), "mx"),
        P(("my", "dp"), "mx"),
        P(("my", "dp"), "mx"),
    )
    return jax.shard_map(body, mesh=mesh, in_specs=in_specs, out_specs=out_specs, check_vma=False)
```

```python
import functools

import jax
import jax.numpy as jnp
from jax import lax
from jax.experimental import pallas as pl
from jax.experimental.pallas import tpu as pltpu
from jax.sharding import PartitionSpec as P

PATCHES = 256
NZ = 8
NY = 4
INV_ROOT2 = 0.7071067811865476
INV_ROOT2PI = 0.3989422804014327
FIRST_FIX = 1.0 - 0.9**10
SECOND_FIX = 1.0 - 0.99**10
BF16 = jnp.bfloat16
F32 = jnp.float32
VMEM_BYTES = 24 * 1024 * 1024
WHOLE_VMEM_BYTES = 63 * 1024 * 1024


def swap_core(value):
    return lax.ppermute(value, "dp", [(i, i ^ 1) for i in range(4)])


def swap_x_lo(value):
    return lax.ppermute(value, "dp", [(i, i ^ 2) for i in range(4)])


def swap_x_hi(value):
    return lax.ppermute(value, "mx", [(i, i ^ 1) for i in range(16)])


def swap_x_both(value):
    pairs = [(d * 16 + m, (d ^ 2) * 16 + (m ^ 1)) for d in range(4) for m in range(16)]
    return lax.ppermute(value, ("dp", "mx"), pairs)


def shift_z(value, by):
    return lax.ppermute(value, "mx", [(i, (i + 2 * by) % 16) for i in range(16)])


def shift_y(value, by):
    return lax.ppermute(value, "my", [(i, (i + by) % NY) for i in range(NY)])


def vmem_specs(count):
    return [pl.BlockSpec(memory_space=pltpu.VMEM)] * count


def call_kernel(kernel, out_shapes, operands, scratch=(), flops=0, scalars=None, follows=()):
    operands, follows = list(operands), list(follows)
    moved = sum(o.size * o.dtype.itemsize for o in operands)
    moved += sum(o.size * o.dtype.itemsize for o in out_shapes)
    in_specs = vmem_specs(len(operands))
    in_specs += [pl.BlockSpec(memory_space=pl.ANY)] * len(follows)
    skip, count = len(operands), len(follows)
    operands += follows
    if scalars is not None:
        in_specs = [pl.BlockSpec(memory_space=pltpu.SMEM)] + in_specs
        operands = [scalars] + operands
        skip += 1

    def run(*refs):
        kernel(*refs[:skip], *refs[skip + count :])

    return pl.pallas_call(
        run,
        out_shape=out_shapes,
        in_specs=in_specs,
        out_specs=vmem_specs(len(out_shapes)),
        scratch_shapes=list(scratch),
        compiler_params=pltpu.CompilerParams(vmem_limit_bytes=VMEM_BYTES),
        cost_estimate=pl.CostEstimate(flops=0, bytes_accessed=0, transcendentals=0),
    )(*operands)


def like(array, shape=None, dtype=None):
    return jax.ShapeDtypeStruct(shape or array.shape, dtype or array.dtype)


def copy_all(pairs, sems):
    copies = [pltpu.make_async_copy(src, dst, sems.at[i]) for i, (src, dst) in enumerate(pairs)]
    for copy in copies:
        copy.start()
    for copy in copies:
        copy.wait()


def copy_kernel(kernel, out_shapes, place, operands, copies, follows=(), vmem=VMEM_BYTES):
    count = len(operands)

    def run(place_ref, *refs):
        kernel(place_ref, *refs[:count], *refs[count + len(follows) :])

    return pl.pallas_call(
        run,
        out_shape=out_shapes,
        in_specs=[pl.BlockSpec(memory_space=pltpu.SMEM)]
        + [pl.BlockSpec(memory_space=pltpu.HBM)] * count
        + [pl.BlockSpec(memory_space=pl.ANY)] * len(follows),
        out_specs=vmem_specs(len(out_shapes)),
        scratch_shapes=[pltpu.SemaphoreType.DMA((copies,))],
        compiler_params=pltpu.CompilerParams(vmem_limit_bytes=vmem),
        cost_estimate=pl.CostEstimate(flops=0, bytes_accessed=0, transcendentals=0),
    )(place, *operands, *follows)


def halves_of(weight, axis, size, x_hi):
    views = []
    for which in (x_hi, 1 - x_hi):
        half = pl.ds(pl.multiple_of(which * size, size), size)
        views.append(weight.at[half, :] if axis == 0 else weight.at[:, half])
    return views


def quarter_kernel(place, tokens, cotangent, pair, sems):
    rows = pair.shape[1]
    line = pl.ds(pl.multiple_of(place[1] * rows, rows), rows)
    copy_all([(tokens.at[line, :], pair.at[0]), (cotangent.at[line, :], pair.at[1])], sems)


def half_kernel(place, w_in, w_out, keep, send, sems):
    size = keep.shape[1]
    stays_in, goes_in = halves_of(w_in, 1, size, place[2])
    stays_out, goes_out = halves_of(w_out, 0, size, place[2])
    copy_all(
        [
            (goes_in, send.at[0]),
            (goes_out, send.at[1]),
            (stays_in, keep.at[0]),
            (stays_out, keep.at[1]),
        ],
        sems,
    )


def forward_kernel(before, beyond, up, down):
    size = up.shape[0]
    up[...] = before[:size]
    down[...] = beyond[size:]


def stack_kernel(one, two, three, send, out, passed):
    for array in range(2):
        for p, source in enumerate((one, two, three)):
            out[3 * array + p] = source[array]
    passed[...] = send[...]


def add_kernel(moving, mine, out):
    out[...] = (moving[...].astype(F32) + mine[...].astype(F32)).astype(BF16)


def add_rounded(moving, mine, follows=()):
    return call_kernel(add_kernel, [like(mine)], [moving, mine], follows=follows)[0]


def act_kernel(pre_own, pre_far, pre_near, back_own, back_far, back_near, out):
    pre_act = pre_own[...].astype(F32) + pre_far[...].astype(F32) + pre_near[...].astype(F32)
    act_back = back_own[...].astype(F32) + back_far[...].astype(F32) + back_near[...].astype(F32)
    value, slope = gelu_pair(pre_act)
    out[0] = value.astype(BF16)
    out[1] = (act_back * slope).astype(BF16)


def half_of(chunk, which):
    return chunk[which] if len(chunk.shape) == 3 else chunk[...]


def assemble_tokens(place, own, moved, first, whole, rows, width):
    z, y = place[0], place[1]
    step = rows // NZ

    def put(c, side, yy, right, block):
        k = lax.rem(c + NZ - z, NZ)
        at = pl.multiple_of(((k * 2 + side) * NY + yy) * step, step)
        columns = slice(width, 2 * width) if right else slice(0, width)
        whole[pl.ds(at, step), columns] = block

    for c in range(NZ):
        for yy in range(NY):
            put(c, 0, yy, False, own[yy * rows + c * step : yy * rows + (c + 1) * step, :])
        line = slice(c * step, (c + 1) * step)
        for j in range(NY):
            yy = lax.rem(y + j, NY)
            skip = 0 if moved[j].shape[0] == 3 else first
            put(c, 1, yy, False, moved[j][skip, line, :])
            put(c, 1, yy, True, moved[j][skip + 1, line, :])
            put(c, 0, yy, True, moved[j][skip + 2, line, :])


def partial_kernel(by_rows, place, own, *refs):
    moved, sources = refs[:NY], refs[NY : NY + 4]
    out, (whole, weight) = refs[NY + 4 : -2], refs[-2:]
    which = 0 if by_rows else 1
    rows, width = own.shape[0] // NY, own.shape[1]
    hid = sources[0].shape[2] if by_rows else sources[0].shape[1]
    assemble_tokens(place, own, moved, 3 * which, whole, rows, width)
    for d in range(2):
        columns = slice(d * width, (d + 1) * width)
        for f in range(2):
            units = slice(f * hid, (f + 1) * hid)
            weight[(columns, units) if by_rows else (units, columns)] = sources[2 * d + f][which]
    contract = (((1,), (0,)), ((), ())) if by_rows else (((1,), (1,)), ((), ()))
    for k in range(0, NZ, 2):
        rows_k = slice(k * rows, (k + 2) * rows)
        both = lax.dot_general(whole[rows_k, :], weight[...], contract, preferred_element_type=F32)
        out[k][...] = both[:rows].astype(BF16)
        out[k + 1][...] = both[rows:].astype(BF16)


def partial_sums(by_rows, place, own, moved, weights, follows=()):
    rows, width = own.shape[0] // NY, own.shape[1]
    hid = weights[0].shape[2 if by_rows else 1]
    outs = [jax.ShapeDtypeStruct((rows, 2 * hid), BF16)] * NZ + [
        jax.ShapeDtypeStruct((NZ * rows, 2 * width), BF16),
        jax.ShapeDtypeStruct((2 * width, 2 * hid) if by_rows else (2 * hid, 2 * width), BF16),
    ]
    flops = 2 * NZ * rows * 2 * width * 2 * hid

    def kernel(*refs):
        partial_kernel(by_rows, *refs)

    results = call_kernel(kernel, outs, [own, *moved, *weights], [], flops, place, follows)
    return results[:NZ], results[NZ], results[NZ + 1]


def grad_kernel(scale, tokens_left, *refs):
    chunks, tokens, outs, whole = refs[:NZ], refs[NZ], refs[NZ + 1 : NZ + 3], refs[NZ + 3]
    rows = chunks[0].shape[1]
    for k in range(NZ):
        whole[k * rows : (k + 1) * rows, :] = half_of(chunks[k], 1 if tokens_left else 0)
    width, hid = outs[0].shape[1:] if tokens_left else outs[0].shape[:0:-1]
    over = (((0,), (0,)), ((), ()))
    for d in range(2):
        for f in range(2):
            units = whole[:, f * hid : (f + 1) * hid]
            columns = tokens[:, d * width : (d + 1) * width]
            left, right = (columns, units) if tokens_left else (units, columns)
            total = lax.dot_general(left, right, over, preferred_element_type=F32)
            outs[f][d] = (total * scale).astype(BF16)


def weight_grad(tokens_left, scale, chunks, tokens, follows=()):
    rows, hid2 = chunks[0].shape[-2:]
    width2 = tokens.shape[1]
    hid, width = hid2 // 2, width2 // 2
    tail = (width, hid) if tokens_left else (hid, width)
    outs = [jax.ShapeDtypeStruct((2,) + tail, BF16)] * 2
    flops = 2 * NZ * rows * hid2 * width2

    def kernel(*refs):
        grad_kernel(scale, tokens_left, *refs)

    scratch = [pltpu.VMEM((NZ * rows, hid2), BF16)]
    return call_kernel(kernel, outs, [*chunks, tokens], scratch, flops, follows=follows)


def back_kernel(count, place, *refs):
    chunks, weight = refs[:count], refs[count]
    outs, whole, total = refs[count + 1 : count + 1 + NY], refs[-2], refs[-1]
    y = place[1]
    rows = chunks[0].shape[-2]
    step = rows // NZ
    width = outs[0].shape[3]
    for k in range(count):
        whole[k * rows : (k + 1) * rows, :] = half_of(chunks[k], 1)
    total[...] = lax.dot_general(
        whole[...], weight[...], (((1,), (1,)), ((), ())), preferred_element_type=F32
    ).astype(BF16)
    for j in range(NY):
        yy = lax.rem(y + j, NY)
        for k in range(count):
            for side in range(2):
                at = pl.multiple_of(((k * 2 + side) * NY + yy) * step, step)
                line = slice(k * step, (k + 1) * step)
                for d in range(2):
                    columns = slice(d * width, (d + 1) * width)
                    outs[j][side, d, line, :] = total[pl.ds(at, step), columns]


def token_grad(place, chunks, weight, follows=()):
    count = len(chunks)
    rows, hid2 = chunks[0].shape[-2:]
    width2 = weight.shape[0]
    outs = [jax.ShapeDtypeStruct((2, 2, count * rows // NZ, width2 // 2), BF16)] * NY
    flops = 2 * count * rows * hid2 * width2
    scratch = [pltpu.VMEM((count * rows, hid2), BF16), pltpu.VMEM((count * rows, width2), BF16)]

    def kernel(*refs):
        back_kernel(count, *refs)

    return call_kernel(kernel, outs, [*chunks, weight], scratch, flops, place, follows)


def send_over_y(outs):
    return [outs[0], shift_y(outs[1], 1), shift_y(outs[2], 2), shift_y(outs[3], 3)]


def sum_kernel(*refs):
    terms, outs = refs[:-4], refs[-4:]
    at = 0
    for group in (terms[:NY], terms[NY:]):
        size = group[0].shape[2]
        for side in range(2):
            for d in range(2):
                total = sum(term[side, d].astype(F32) for term in group)
                out = outs[side * 2 + d]
                out[at : at + size, :] = total.astype(out.dtype)
        at += size


def place_kernel(order, place, own, one, two, three, out):
    z = place[0]
    step = out.shape[0] // NZ
    for i, k in enumerate(order):
        line = slice(i * step, (i + 1) * step)
        total = own[line, :] + one[line, :].astype(F32)
        total += two[line, :].astype(F32) + three[line, :].astype(F32)
        at = pl.multiple_of(lax.rem(z + k, NZ) * step, step)
        out[pl.ds(at, step), :] = total.astype(BF16)


def gelu_pair(pre_act):
    cumulative = 0.5 * (1.0 + jax.scipy.special.erf(pre_act * INV_ROOT2))
    density = jnp.exp(-0.5 * pre_act * pre_act) * INV_ROOT2PI
    return (pre_act * cumulative, cumulative + pre_act * density)


def leave_kernel(kept, moved, out):
    out[...] = (kept[1].astype(F32) + moved[1].astype(F32)).astype(BF16)


def adam_kernel(axis, place, kept, moved, there, first, second, step_dir, new_first, new_second, mark):
    mark[...] = jnp.zeros_like(mark)
    size = there.shape[axis]
    rows = there.shape[0]
    block = rows // ADAM_STEPS
    for local, which in ((True, place[2]), (False, 1 - place[2])):
        start = pl.multiple_of(which * size, size)
        for step in range(ADAM_STEPS):
            line = slice(step * block, (step + 1) * block)
            if local:
                grad = kept[0, line, :].astype(F32) + moved[0, line, :].astype(F32)
            else:
                grad = there[line, :].astype(F32)
            at = (pl.ds(start + step * block, block), slice(None))
            if axis == 1:
                at = (line, pl.ds(start, size))
            first_new = 0.9 * first[at] + 0.1 * grad
            second_new = 0.99 * second[at] + 0.01 * grad * grad
            new_first[at] = first_new
            new_second[at] = second_new
            scaled = second_new * (1.0 / SECOND_FIX)
            scaled = scaled * lax.rsqrt(scaled) + 1e-08
            step_dir[at] = (first_new * (1.0 / FIRST_FIX) / scaled).astype(BF16)


ADAM_STEPS = 4


def adam_step(axis, place, kept, moved, there, first, second, follows=()):
    return call_kernel(
        functools.partial(adam_kernel, axis),
        [like(first, dtype=BF16), like(first), like(first), like(first, (8, 128))],
        [kept, moved, there, first, second],
        scalars=place,
        follows=follows,
    )


def reduce_over_z(parts, long_way, follows=()):
    far = parts[4]
    sums = []
    order = (5, 6, 7) if long_way < 0 else (3, 2, 1)
    for i, k in enumerate(order):
        far = add_rounded(shift_z(far, long_way), parts[k], [f for f in follows[i : i + 1] if f is not None])
        sums.append(far)
    far = shift_z(far, long_way)
    order = (3, 2, 1) if long_way < 0 else (5, 6, 7)
    near = parts[order[0]]
    for k in order[1:]:
        near = add_rounded(shift_z(near, -long_way), parts[k])
    near = shift_z(near, -long_way)
    return (parts[0], far, near), sums


def gather_over_z(chunk):
    found = [chunk] + [None] * (NZ - 1)
    for step in range(1, 4):
        found[step] = shift_z(found[step - 1], -1)
        found[-step] = shift_z(found[(1 - step) % NZ], 1)
    cotangents = shift_z(found[3][1], -1)
    acts = shift_z(found[5][0], 1)
    return found[:4] + [acts] + found[5:], found[:4] + [cotangents] + found[5:]


def body(normed, out_grad, w_in, w_out, first_in, second_in, first_out, second_out):
    mx = lax.axis_index("mx")
    y = lax.axis_index("my")
    z, x_hi = mx // 2, mx % 2
    place = jnp.stack([z, y, x_hi]).astype(jnp.int32)
    rows = normed.shape[0] // NY
    width, hid = w_in.shape[0], w_in.shape[1] // 2

    (pair,) = copy_kernel(
        quarter_kernel,
        [like(normed, (2, rows, width))],
        place,
        [normed, out_grad],
        2,
        vmem=WHOLE_VMEM_BYTES,
    )
    keep, send = copy_kernel(half_kernel, [like(w_in, (2, width, hid))] * 2, place, [w_in, w_out], 4)
    mine, send = call_kernel(
        stack_kernel,
        [like(normed, (6, rows, width)), like(send)],
        [swap_x_lo(pair), swap_x_both(pair), swap_x_hi(pair), send],
    )
    part = swap_x_hi(send)
    above, below = shift_y(mine, -1), shift_y(mine, 1)
    up, down = call_kernel(
        forward_kernel, [like(normed, (3, rows, width))] * 2, [below, above]
    )
    weights = [keep, swap_core(keep), part, swap_core(part)]
    pre_parts, whole_in, weight_in = partial_sums(
        True, place, normed, [mine, above, shift_y(up, 1), below], weights
    )
    back_parts, whole_out, _ = partial_sums(
        False, place, out_grad, [mine, above, shift_y(down, -1), below], weights, [pre_parts[4]]
    )
    back_terms, back_sums = reduce_over_z(back_parts, 1)
    pre_terms, _ = reduce_over_z(pre_parts, -1, [None, back_parts[4], back_sums[0]])
    shape = (2,) + pre_parts[0].shape
    (chunk,) = call_kernel(act_kernel, [like(normed, shape)], [*pre_terms, *back_terms])
    acts, act_grads = gather_over_z(chunk)

    images = float(normed.shape[0] * lax.axis_size("dp") // PATCHES)
    first_places, last_places = (0, 1, 7, 2, 6), (3, 5, 4)
    early = token_grad(place, [act_grads[k] for k in first_places], weight_in)
    terms = send_over_y(early)
    kept_out, swapped = weight_grad(False, 1.0 / images, acts, whole_out, terms[1:])
    moved_out = swap_core(swapped)
    kept_in, swapped = weight_grad(True, 1.0 / images, act_grads, whole_in)
    moved_in = swap_core(swapped)
    late = token_grad(
        place, [act_grads[k] for k in last_places], weight_in, [kept_in]
    )
    terms += send_over_y(late)
    leaving_out = call_kernel(
        leave_kernel, [like(w_out, (hid, width))], [kept_out, moved_out], follows=late[:1]
    )[0]
    there_out = swap_x_hi(leaving_out)
    leaving_in = call_kernel(
        leave_kernel, [like(swapped, (width, hid))], [kept_in, moved_in], follows=[leaving_out]
    )[0]
    there_in = swap_x_hi(leaving_in)
    block = (rows, width)
    own, side, other_side, both = call_kernel(
        sum_kernel, [like(normed, block, F32)] + [like(normed, block)] * 3, terms
    )
    update_out, new_first_out, new_second_out, mark = adam_step(
        0, place, kept_out, moved_out, there_out, first_out, second_out, [own]
    )
    update_in, new_first_in, new_second_in, mark = adam_step(
        1, place, kept_in, moved_in, there_in, first_in, second_in, [mark]
    )
    input_grad = call_kernel(
        functools.partial(place_kernel, first_places + last_places),
        [like(normed, block)],
        [own, swap_x_lo(other_side), swap_x_hi(side), swap_x_both(both)],
        scalars=place,
        follows=[mark],
    )[0]
    return (
        input_grad,
        update_in,
        new_first_in,
        new_second_in,
        update_out,
        new_first_out,
        new_second_out,
    )


def solution(mesh):
    in_specs = (
        P("dp", "mx"),
        P("dp", "mx"),
        P("mx", ("my", "dp")),
        P(("my", "dp"), "mx"),
        P("mx", ("my", "dp")),
        P("mx", ("my", "dp")),
        P(("my", "dp"), "mx"),
        P(("my", "dp"), "mx"),
    )
    out_specs = (
        P(("dp", "my"), "mx"),
        P("mx", ("my", "dp")),
        P("mx", ("my", "dp")),
        P("mx", ("my", "dp")),
        P(("my", "dp"), "mx"),
        P(("my", "dp"), "mx"),
        P(("my", "dp"), "mx"),
    )
    return jax.shard_map(body, mesh=mesh, in_specs=in_specs, out_specs=out_specs, check_vma=False)
```
